512 devices in a mesh: gy: 32 (over y, x), gz: 16 (over z, core).
Axes of the slice: x: 4, y: 8, z: 8, core: 2. Of those that a mesh axis runs over, the one named last changes fastest.
Arguments:
- rhs: float32 [5, 4, 64, 32, 128], P(None, None, 'gy', 'gz'), may hold values from -6 to 6
- bc_codes: int32 [4, 64, 32, 128], P(None, 'gy', 'gz'), may hold values from 0 to 2
- line_pivots: float32 [5, 5, 4, 64, 32, 128], P(None, None, None, 'gy', 'gz'), may hold values from -0.6 to 1.4
- x_lower: float32 [5, 5, 3, 64, 32, 128], P(None, None, None, 'gy', 'gz'), may hold values from -0.9 to 0.9
- x_upper: float32 [5, 5, 3, 64, 32, 128], P(None, None, None, 'gy', 'gz'), may hold values from -0.9 to 0.9
- lower_coupling: float32 [2, 5, 5, 4, 64, 32, 128], P(None, None, None, None, 'gy', 'gz'), may hold values from -0.54 to 0.15
- upper_coupling: float32 [2, 5, 5, 4, 64, 32, 128], P(None, None, None, None, 'gy', 'gz'), may hold values from -0.54 to 0.15
- cell_volume: float32 [64, 32], P('gy', 'gz'), may hold values from 0.05 to 0.5
Outputs:
- correction: float32 [5, 4, 64, 32, 128], P(None, None, 'gy', 'gz')
- coarse_residual: float32 [5, 4, 64, 128], P(None, None, 'gy', 'gz')
The draws below stay inside these ranges and needn't reach their ends.
All inputs are finite; a program needn't handle non-finite values.
Results may differ from the reference program's by a relative error of at most 0.00012.
Values sent between devices are 32-bit elements; how exact they have to be, the bound alone decides.
No kernel may reach another device: no remote copies, remote signals or barrier semaphores. Data moves between devices by JAX's collectives and lax.ppermute only.
A program may use at most 64 MiB of HBM per device.

```python
import math
import jax
import jax.numpy as jnp
from jax import lax

NVAR = 5
PLANES = 4
ITERS = 2
SLABS = 128
NY = 64
NZ = 32


def draw_line_pivots(key, part):
    key = jax.random.fold_in(key, 11)
    key_off, key_diag = jax.random.split(key)
    shape = (5, 5, PLANES, NY, NZ, SLABS)
    off_values = jnp.clip(0.15 * jax.random.normal(key_off, shape, jnp.float32), -0.6, 0.6)
    diag_values = jnp.exp(jax.random.uniform(key_diag, shape, jnp.float32, jnp.log(0.6), jnp.log(1.4)))
    row_index = lax.broadcasted_iota(jnp.int32, shape, 0)
    column_index = lax.broadcasted_iota(jnp.int32, shape, 1)
    return jnp.where(row_index == column_index, diag_values, off_values)


def leading_channels(key):
    order = jax.random.permutation(jax.random.fold_in(key, 7), 5)
    return order < 3


def assemble_blocks(strong_rows, strong_values, off_values, shape):
    row_index = lax.broadcasted_iota(jnp.int32, shape, 1)
    column_index = lax.broadcasted_iota(jnp.int32, shape, 2)
    row_strong = strong_rows[None, :, None, None, None, None, None]
    diag_values = -jnp.where(row_strong, strong_values, 0.08 * strong_values)
    return jnp.where(row_index == column_index, diag_values, off_values)


def draw_lower_coupling(key, part):
    strong_rows = leading_channels(key)
    key = jax.random.fold_in(key, 21)
    key_off, key_diag = jax.random.split(key)
    shape = (2, 5, 5, PLANES, NY, NZ, SLABS)
    off_values = jnp.clip(0.04 * jax.random.normal(key_off, shape, jnp.float32), -0.15, 0.15)
    strong_values = jax.random.uniform(key_diag, shape, jnp.float32, 0.42, 0.54)
    return assemble_blocks(strong_rows, strong_values, off_values, shape)


def draw_upper_coupling(key, part):
    strong_rows = jnp.logical_not(leading_channels(key))
    key = jax.random.fold_in(key, 22)
    key_off, key_diag = jax.random.split(key)
    shape = (2, 5, 5, PLANES, NY, NZ, SLABS)
    off_values = jnp.clip(0.04 * jax.random.normal(key_off, shape, jnp.float32), -0.15, 0.15)
    strong_values = jax.random.uniform(key_diag, shape, jnp.float32, 0.42, 0.54)
    return assemble_blocks(strong_rows, strong_values, off_values, shape)


def touch_ends(array, stream_key, smallest, high):
    spot = [jax.random.randint(jax.random.fold_in(stream_key, axis), (), 0, length) for axis, length in enumerate(array.shape)]
    main_axis = array.shape.index(max(array.shape))
    next_to = spot[:main_axis] + [(spot[main_axis] + 1) % array.shape[main_axis]] + spot[main_axis + 1:]
    return array.at[tuple(spot)].set(smallest).at[tuple(next_to)].set(high)


def block_scale(stream_key, dims, pieces, smallest, top_value):
    loudness = 1.0
    for dim, parts in pieces:
        heights = jax.random.uniform(jax.random.fold_in(jax.random.fold_in(stream_key, 6), dim), (parts,), jnp.float32, smallest / len(pieces), top_value / len(pieces))
        loudness = loudness * jnp.repeat(jnp.exp(heights), dims[dim] // parts).reshape((-1,) + (1,) * (len(dims) - 1 - dim))
    return loudness


def normal_values(key, extent, scale, bound, pieces=(), kind=jnp.bfloat16):
    values = jax.random.normal(key, extent, jnp.float32) * scale
    if len(pieces) > 0:
        values = block_scale(key, extent, pieces, -0.22, 0.18) * values
    return jnp.clip(values, min=-bound, max=bound).astype(kind)


def setup_inputs(seed: int = 0) -> dict:
    splits = jax.random.split(jax.random.key(seed), 9)
    rhs = normal_values(splits[0], (NVAR, PLANES, NY, NZ, SLABS), 1.0, 6.0, ((2, 32), (3, 16)), jnp.float32)
    bc_codes = touch_ends(jax.random.randint(splits[1], (PLANES, NY, NZ, SLABS), 0, 3), jax.random.fold_in(splits[1], 1), 0, 2).astype(jnp.int32)
    line_pivots = draw_line_pivots(jax.random.fold_in(splits[8], 71), 0)
    x_lower = normal_values(splits[3], (NVAR, NVAR, PLANES - 1, NY, NZ, SLABS), 0.15, 0.9, ((3, 32), (4, 16)), jnp.float32)
    x_upper = normal_values(splits[4], (NVAR, NVAR, PLANES - 1, NY, NZ, SLABS), 0.15, 0.9, ((3, 32), (4, 16)), jnp.float32)
    lower_coupling = draw_lower_coupling(jax.random.fold_in(splits[8], 71), 0)
    upper_coupling = draw_upper_coupling(jax.random.fold_in(splits[8], 71), 0)
    cell_volume = jnp.clip(jnp.exp(math.log(0.5) - 2.3025851 * jax.random.uniform(splits[7], (NY, NZ), jnp.float32) ** block_scale(splits[7], (NY, NZ), ((0, 32), (1, 16)), -0.2, 0.2)), 0.05, 0.5)
    return {"rhs": rhs, "bc_codes": bc_codes, "line_pivots": line_pivots, "x_lower": x_lower, "x_upper": x_upper, "lower_coupling": lower_coupling, "upper_coupling": upper_coupling, "cell_volume": cell_volume}


def apply_block(matrix, vector):
    return jnp.sum(matrix * vector[None], axis=1)


def line_solve(pivots, x_lower, x_upper, source):
    forward_values = []
    for plane in range(PLANES):
        current = source[:, plane]
        if plane > 0:
            current = current - apply_block(x_lower[:, :, plane - 1], forward_values[plane - 1])
        forward_values.append(apply_block(pivots[:, :, plane], current))
    solved = [None] * PLANES
    solved[PLANES - 1] = forward_values[PLANES - 1]
    for plane in range(PLANES - 2, -1, -1):
        solved[plane] = forward_values[plane] - apply_block(pivots[:, :, plane], apply_block(x_upper[:, :, plane], solved[plane + 1]))
    return jnp.stack(solved, axis=1)


def masked_source(rhs, bc_codes):
    component = lax.broadcasted_iota(jnp.int32, (5, 1, 1, 1, 1), 0)
    wall = (bc_codes == 1)[None]
    symmetry = (bc_codes == 2)[None]
    removed = (wall & (component >= 1) & (component <= 3)) | (symmetry & (component == 3))
    return jnp.where(removed, jnp.zeros_like(rhs), rhs)


def shifted(values_in, axis, offset):
    length = values_in.shape[axis]
    zero_rim = jnp.zeros_like(lax.slice_in_dim(values_in, 0, 1, axis=axis))
    if offset == 1:
        return jnp.concatenate([zero_rim, lax.slice_in_dim(values_in, 0, length - 1, axis=axis)], axis=axis)
    return jnp.concatenate([lax.slice_in_dim(values_in, 1, length, axis=axis), zero_rim], axis=axis)


def neighbor_terms(values_in, coupling, offset):
    return apply_block(coupling[0], shifted(values_in, 2, offset)) + apply_block(coupling[1], shifted(values_in, 3, offset))


def to_front(array_in):
    return jnp.moveaxis(array_in, (array_in.ndim - 3, array_in.ndim - 2), (0, 1))


def sweep(source_terms, couple_y, couple_z, pivots, x_lower, x_upper):
    moved = [to_front(item) for item in (source_terms, couple_y, couple_z, pivots, x_lower, x_upper)]
    cells_z = source_terms.shape[3]
    slabs = source_terms.shape[4]

    def row_step(previous_row, row_inputs):
        def cell_step(left_value, cell_inputs):
            source_here, matrix_y, matrix_z, pivot_here, lower_here, upper_here, above_value = cell_inputs
            current = source_here - apply_block(matrix_y, above_value) - apply_block(matrix_z, left_value)
            solved = line_solve(pivot_here, lower_here, upper_here, current)
            return solved, solved

        start_value = jnp.zeros((5, PLANES, slabs), jnp.float32)
        unused, row_values = lax.scan(cell_step, start_value, tuple(row_inputs) + (previous_row,))
        return row_values, row_values

    first_row = jnp.zeros((cells_z, 5, PLANES, slabs), jnp.float32)
    unused, swept = lax.scan(row_step, first_row, tuple(moved))
    return jnp.moveaxis(swept, (0, 1), (2, 3))


def flipped(array_in):
    return jnp.flip(array_in, axis=(array_in.ndim - 3, array_in.ndim - 2))


def reference(rhs, bc_codes, line_pivots, x_lower, x_upper, lower_coupling, upper_coupling, cell_volume):
    source = masked_source(rhs, bc_codes)
    correction = jnp.zeros_like(source)
    forward_pass = source
    for iteration in range(ITERS):
        if iteration == 0:
            forward_source = source
        else:
            forward_source = source - neighbor_terms(correction, upper_coupling, -1)
        forward_pass = sweep(forward_source, lower_coupling[0], lower_coupling[1], line_pivots, x_lower, x_upper)
        backward_source = source - neighbor_terms(forward_pass, lower_coupling, 1)
        backward_pass = sweep(flipped(backward_source), flipped(upper_coupling[0]), flipped(upper_coupling[1]), flipped(line_pivots), flipped(x_lower), flipped(x_upper))
        correction = flipped(backward_pass)
    residual = neighbor_terms(forward_pass - correction, lower_coupling, 1)
    coarse_residual = jnp.sum(cell_volume[None, None, :, :, None] * residual, axis=3)
    return correction, coarse_residual
```

```python
import jax
import jax.numpy as jnp
from jax import lax
from jax.experimental import pallas as pl
from jax.experimental.pallas import tpu as pltpu
from jax.sharding import Mesh, PartitionSpec as P

F32 = jnp.float32
NZ = 32
NY = 64
DIAGS = NY + NZ - 1
PITCH = 272
SWAP = [(0, 1), (1, 0)]
GROUP = ("z", "cy", "xh")
SMEM = pltpu.SMEM
VMEM = pltpu.VMEM


def tree(terms):
    terms = list(terms)
    while len(terms) > 1:
        terms = [
            terms[k] + terms[k + 1] if k + 1 < len(terms) else terms[k]
            for k in range(0, len(terms), 2)
        ]
    return terms[0]


def spread(value, i):
    return jnp.broadcast_to(value[i : i + 1, :], (8, 128))


def pack_kernel(meta, vol, rhs, codes, piv, low_x, up_x, low, up, out, tile):
    first_z = meta[2]
    last_z = meta[3]
    zero = jnp.zeros((25, 128), F32)
    component = lax.broadcasted_iota(jnp.int32, (5, 128), 0)
    for jz in range(2):
        for jy in range(2):
            for p in range(4):
                at = p * 4 + jy * 2 + jz
                t = tile.at[(jy * 4 + p) % 2]
                t[0:25, :] = piv[pl.ds(at, 25, stride=16), :]
                t[25:50, :] = low_x[pl.ds(at - 4, 25, stride=12), :] if p > 0 else zero
                t[50:75, :] = up_x[pl.ds(at, 25, stride=12), :] if p < 3 else zero
                t[75:100, :] = low[pl.ds(at, 25, stride=16), :]
                along_z = low[pl.ds(400 + at, 25, stride=16), :]
                if jz == 0:
                    along_z = jnp.where(first_z == 1, 0.0, along_z)
                t[100:125, :] = along_z
                t[125:128, :] = zero[:3]
                out[pl.ds(jz * 8 + jy * 4 + p, 128, stride=24), :] = t[...].T
    for jz in range(2):
        for p in range(4):
            t = tile.at[p % 2]
            for jy in range(2):
                at = p * 4 + jy * 2 + jz
                base = 64 * jy
                t[base : base + 25, :] = up[pl.ds(at, 25, stride=16), :]
                along_z = up[pl.ds(400 + at, 25, stride=16), :]
                if jz == 1:
                    along_z = jnp.where(last_z == 1, 0.0, along_z)
                t[base + 25 : base + 50, :] = along_z
                code = jnp.broadcast_to(codes[at : at + 1, :], (5, 128))
                removed = ((code == 1) & (component >= 1) & (component <= 3)) | (
                    (code == 2) & (component == 3)
                )
                t[base + 50 : base + 55, :] = jnp.where(
                    removed, 0.0, rhs[pl.ds(at, 5, stride=16), :]
                )
                t[base + 55 : base + 64, :] = jnp.full((9, 128), vol[jy, jz], F32)
            out[pl.ds(16 + jz * 4 + p, 128, stride=24), :] = t[...].T


def column(ref, d, base, j):
    return ref[d, pl.ds(base + j, 8, stride=5), :]


def row(ref, d, r):
    return jnp.broadcast_to(ref[d, pl.ds(r, 1), :], (8, 128))


def main_kernel(
    meta, q0, q1, q2, q3, out, df, du, tf, tu, tmp, al, au, g, vv, f1, c1, rl, ru, sem
):
    core = meta[0]
    side = meta[1]
    copies = []
    for n, (q, dc, dx) in enumerate(((q0, 0, 0), (q1, 1, 0), (q2, 0, 1), (q3, 1, 1))):
        c = core + dc - 2 * core * dc
        x = side + dx - 2 * side * dx
        for part in range(3):
            src = q.at[:, :, pl.ds(8 * part, 8), :]
            dst = (
                df.at[:, c, part, pl.ds(0, 16), x] if part < 2 else du.at[:, c, pl.ds(0, 16), x]
            )
            copies.append(pltpu.make_async_copy(src, dst, sem.at[n * 3 + part]))
    for copy in copies:
        copy.start()
    for copy in copies:
        copy.wait()
    fl = df.reshape(32 * PITCH, 128)
    ul = du.reshape(16 * PITCH, 128)
    lane = lax.broadcasted_iota(jnp.int32, (8, 128), 1)
    sub = lax.broadcasted_iota(jnp.int32, (8, 128), 0)
    z = lane & 31
    even_z = (lane & 1) == 0

    def turn_f(d, carry):
        block = jnp.concatenate(
            [fl[pl.ds(4 * d + p, 32, stride=PITCH - 4), :] for p in range(4)], axis=0
        )
        tf[d, pl.ds(0, 128), :] = block.T
        return carry

    lax.fori_loop(0, DIAGS, turn_f, 0, unroll=5)

    def turn_u(e, carry):
        for p in range(4):
            for jz in range(2):
                tmp[pl.ds(p * 32 + jz, 16, stride=2), :] = ul[
                    pl.ds(8 * e + jz * 4 + p, 16, stride=PITCH - 8), :
                ]
        tu[pl.ds(pl.multiple_of(128 * e + 128, 128), 128), :] = tmp[...].T
        return carry

    lax.fori_loop(0, 47, turn_u, 0)

    def prepare(d, carry):
        piv = [column(tf, d, 0, i) for i in range(5)]
        pl_cols = [tree([piv[i] * row(tf, d, 25 + 5 * i + j) for i in range(5)]) for j in range(5)]
        pu_cols = [tree([piv[i] * row(tf, d, 50 + 5 * i + j) for i in range(5)]) for j in range(5)]

        def times(left, right):
            return [tree([left[i] * spread(right[j], i) for i in range(5)]) for j in range(5)]

        def shifted(cols, by):
            return [pltpu.roll(v, by, 1) for v in cols]

        w = [piv]
        for _ in range(3):
            w.append([-v for v in times(pl_cols, shifted(w[-1], 32))])
        inverse = {3: w[3]}
        for s in (2, 1, 0, -1, -2, -3):
            below = times(pu_cols, shifted(inverse[s + 1], 96))
            inverse[s] = [w[s][j] - below[j] if s >= 0 else -below[j] for j in range(5)]
        full = [inverse[0]] + [
            [a + b for a, b in zip(inverse[s], inverse[s - 4])] for s in (1, 2, 3)
        ]
        for k in range(7):
            v = tf[d, pl.ds(72 + 8 * k, 8), :]
            for s in range(4):
                rl[s, pl.ds(8 * k, 8), :] = v if s == 0 else pltpu.roll(v, 32 * s, 1)
        for k in range(8):
            even = tu[pl.ds(pl.multiple_of(64 * d + 128, 64) + 8 * k, 8), :]
            odd = tu[pl.ds(pl.multiple_of(64 * d + 64, 64) + 8 * k, 8), :]
            v = jnp.where(even_z, even, odd)
            for s in range(4):
                ru[s, pl.ds(8 * k, 8), :] = v if s == 0 else pltpu.roll(v, 32 * s, 1)
        for s in range(4):
            for n, (dest, source, base) in enumerate(
                ((al, rl, 3), (al, rl, 28), (au, ru, 0), (au, ru, 25))
            ):
                for j in range(5):
                    dest[d, pl.ds(8 * (s * 10 + 5 * (n % 2) + j), 8), :] = tree(
                        [full[s][i] * row(source, s, base + 5 * i + j) for i in range(5)]
                    )
        g[d] = tree([full[s][i] * row(ru, s, 50 + i) for s in range(4) for i in range(5)])
        vv[d] = row(ru, 0, 55)
        return carry

    lax.fori_loop(0, DIAGS, prepare, 0)

    def product(ref, d, f, step):
        terms = []
        for s in range(4):
            by_y = f if s == 0 else pltpu.roll(f, 32 * s, 1)
            by_z = pltpu.roll(f, (32 * s + step) % 128, 1)
            for i in range(5):
                terms.append(ref[d, pl.ds(8 * (s * 10 + i), 8), :] * spread(by_y, i))
            for i in range(5):
                terms.append(ref[d, pl.ds(8 * (s * 10 + 5 + i), 8), :] * spread(by_z, i))
        return tree(terms)

    def inside(d):
        return (z <= d) & (z >= d - (NY - 1))

    nothing = jnp.zeros((8, 128), F32)

    def forward_first(d, f):
        f = jnp.where(inside(d), g[d] - product(al, d, f, 1), 0.0)
        f1[d] = f
        return f

    lax.fori_loop(0, DIAGS, forward_first, nothing)

    def backward_first(n, f):
        d = DIAGS - 1 - n
        coupled = product(au, d, f, -1)
        f = jnp.where(inside(d), f1[d] - coupled, 0.0)
        f1[d] = f
        g[d] = coupled
        return f

    lax.fori_loop(0, DIAGS, backward_first, nothing)

    def forward_second(d, f):
        coupled = product(al, d, f, 1)
        f = jnp.where(inside(d), -(g[d] + coupled), 0.0)
        c1[d] = coupled
        return f

    lax.fori_loop(0, DIAGS, forward_second, nothing)

    def backward_second(n, f):
        d = DIAGS - 1 - n
        coupled = product(au, d, f, -1)
        f = jnp.where(inside(d), -(c1[d] + coupled), 0.0)
        f1[d] = f1[d] + f
        c1[d] = jnp.where(inside(d), coupled, 0.0)
        return f

    lax.fori_loop(0, DIAGS, backward_second, nothing)

    def residual(d, before):
        by_z = pltpu.roll(before, 1, 1)
        g[d] = vv[d] * tree(
            [column(tf, d, 75, i) * spread(before, i) for i in range(5)]
            + [column(tf, d, 100, i) * spread(by_z, i) for i in range(5)]
        )
        return c1[d]

    lax.fori_loop(0, DIAGS, residual, nothing)
    for bit, length in ((16, 79), (8, 71), (4, 67), (2, 65), (1, 64)):

        def straighten(d, carry, bit=bit):
            far = (z & bit) != 0
            f1[d] = jnp.where(far, f1[d + bit], f1[d])
            g[d] = jnp.where(far, g[d + bit], g[d])
            return carry

        lax.fori_loop(0, length, straighten, 0)

    owner_y = lane & 15
    owner_z = lane >> 4

    def collect(n, sums):
        sums = list(sums)
        for jy in range(2):
            y = 4 * n + 2 * side + jy
            value = f1[y]
            total = g[y]
            for by in (16, 8, 4, 2, 1):
                total = total + pltpu.roll(total, 128 - by, 1)
            for jz in range(2):
                merged = jnp.where(sub < 5, value, pltpu.roll(total, 5 if jz == 0 else 2, 0))
                for p in range(4):
                    index = jnp.where(sub < 5, p * 32 + 4 * owner_z + 2 * core + jz, p * 32)
                    picked = jnp.take_along_axis(merged, index, axis=1)
                    k = p * 4 + jz * 2 + jy
                    sums[k] = jnp.where(owner_y == n, picked, sums[k])
        return tuple(sums)

    slots = lax.fori_loop(0, 16, collect, (nothing,) * 16)
    out[...] = jnp.concatenate(slots, axis=0).T


def unpack_kernel(meta, slots, correction, coarse):
    values = slots[...].T
    gz = meta[4]
    for p in range(4):
        for jy in range(2):
            for jz in range(2):
                k = 8 * (p * 4 + jz * 2 + jy)
                correction[pl.ds(p * 4 + jy * 2 + jz, 5, stride=16), :] = values[k : k + 5]
                extra = pltpu.roll(values[k : k + 8], (128 - 8 * gz) % 128, 1)
                if jz == 0:
                    coarse[pl.ds(p * 2 + jy, 3, stride=8), :] = extra[5:8]
                else:
                    coarse[pl.ds(24 + p * 2 + jy, 2, stride=8), :] = extra[5:7]


def on_device(rhs, codes, piv, low_x, up_x, low, up, volume):
    core = lax.axis_index("c")
    side = lax.axis_index("xl")
    gz = lax.axis_index("z") * 2 + core
    meta = jnp.stack(
        [core, side, (gz == 0).astype(jnp.int32), (gz == 15).astype(jnp.int32), gz]
    ).astype(jnp.int32)
    smem = pl.BlockSpec(memory_space=SMEM)
    vmem = pl.BlockSpec(memory_space=VMEM)
    hbm = pl.BlockSpec(memory_space=pl.ANY)
    packed = pl.pallas_call(
        pack_kernel,
        out_shape=jax.ShapeDtypeStruct((128 * 24, 128), F32),
        in_specs=[smem, smem] + [vmem] * 7,
        out_specs=vmem,
        scratch_shapes=[pltpu.VMEM((2, 128, 128), F32)],
        compiler_params=pltpu.CompilerParams(vmem_limit_bytes=32 << 20),
        name="pack",
    )(
        meta,
        volume,
        rhs.reshape(80, 128),
        codes.reshape(16, 128),
        piv.reshape(400, 128),
        low_x.reshape(300, 128),
        up_x.reshape(300, 128),
        low.reshape(800, 128),
        up.reshape(800, 128),
    )
    mine = lax.all_to_all(packed.reshape(128, 24, 128), GROUP, 0, 0, tiled=True)
    other_x = lax.ppermute(mine, "xl", SWAP)
    other_c = lax.ppermute(mine, "c", SWAP)
    other_cx = lax.ppermute(other_x, "c", SWAP)
    quarters = [v.reshape(8, 16, 24, 128) for v in (mine, other_c, other_x, other_cx)]
    diag = pltpu.VMEM((96, 8, 128), F32)
    slots = pl.pallas_call(
        main_kernel,
        out_shape=jax.ShapeDtypeStruct((128, 128), F32),
        in_specs=[smem] + [hbm] * 4,
        out_specs=vmem,
        scratch_shapes=[
            pltpu.VMEM((8, 2, 2, 17, 2, 8, 128), F32),
            pltpu.VMEM((8, 2, 17, 2, 8, 128), F32),
            pltpu.VMEM((DIAGS, 144, 128), F32),
            pltpu.VMEM((50 * 128, 128), F32),
            pltpu.VMEM((128, 128), F32),
            pltpu.VMEM((DIAGS, 320, 128), F32),
            pltpu.VMEM((DIAGS, 320, 128), F32),
            diag,
            diag,
            diag,
            diag,
            pltpu.VMEM((4, 56, 128), F32),
            pltpu.VMEM((4, 64, 128), F32),
            pltpu.SemaphoreType.DMA((12,)),
        ],
        compiler_params=pltpu.CompilerParams(vmem_limit_bytes=60 << 20),
        name="sweeps",
    )(meta, *quarters)
    slots = lax.all_to_all(slots.reshape(128, 1, 128), GROUP, 0, 0, tiled=True)
    correction, coarse = pl.pallas_call(
        unpack_kernel,
        out_shape=(
            jax.ShapeDtypeStruct((80, 128), F32),
            jax.ShapeDtypeStruct((40, 128), F32),
        ),
        in_specs=[smem, vmem],
        out_specs=(vmem, vmem),
        name="unpack",
    )(meta, slots.reshape(128, 128))
    return correction.reshape(5, 4, 2, 2, 128), coarse[:, :8].reshape(5, 4, 2, 8)


def solution(mesh):
    split = Mesh(mesh.devices.reshape(8, 2, 2, 8, 2), ("cy", "xh", "xl", "z", "c"))
    gy = ("cy", "xh", "xl")
    gz = ("z", "c")
    return jax.shard_map(
        on_device,
        mesh=split,
        in_specs=(
            P(None, None, gy, gz, None),
            P(None, gy, gz, None),
            P(None, None, None, gy, gz, None),
            P(None, None, None, gy, gz, None),
            P(None, None, None, gy, gz, None),
            P(None, None, None, None, gy, gz, None),
            P(None, None, None, None, gy, gz, None),
            P(gy, gz),
        ),
        out_specs=(P(None, None, gy, gz, None), P(None, None, gy, gz)),
        check_vma=False,
    )
```

```python
import jax
import jax.numpy as jnp
from jax import lax
from jax.experimental import pallas as pl
from jax.experimental.pallas import tpu as pltpu
from jax.sharding import Mesh, PartitionSpec as P

F32 = jnp.float32
NZ = 32
NY = 64
DIAGS = NY + NZ - 1
PITCH = 272
ROWS = 145
WIDTH = 321
SWAP = [(0, 1), (1, 0)]
GROUP = ("z", "cy", "xh")
SMEM = pltpu.SMEM
VMEM = pltpu.VMEM


def tree(terms):
    terms = list(terms)
    while len(terms) > 1:
        terms = [
            terms[k] + terms[k + 1] if k + 1 < len(terms) else terms[k]
            for k in range(0, len(terms), 2)
        ]
    return terms[0]


def spread(value, i):
    return jnp.broadcast_to(value[i : i + 1, :], (8, 128))


def pack_kernel(meta, vol, rhs, codes, piv, low_x, up_x, low, up, out, tile):
    first_z = meta[2]
    last_z = meta[3]
    zero = jnp.zeros((25, 128), F32)
    component = lax.broadcasted_iota(jnp.int32, (5, 128), 0)
    for jz in range(2):
        for jy in range(2):
            for p in range(4):
                at = p * 4 + jy * 2 + jz
                t = tile.at[(jy * 4 + p) % 2]
                t[0:25, :] = piv[pl.ds(at, 25, stride=16), :]
                t[25:50, :] = low_x[pl.ds(at - 4, 25, stride=12), :] if p > 0 else zero
                t[50:75, :] = up_x[pl.ds(at, 25, stride=12), :] if p < 3 else zero
                t[75:100, :] = low[pl.ds(at, 25, stride=16), :]
                along_z = low[pl.ds(400 + at, 25, stride=16), :]
                if jz == 0:
                    along_z = jnp.where(first_z == 1, 0.0, along_z)
                t[100:125, :] = along_z
                t[125:128, :] = zero[:3]
                out[pl.ds(jz * 8 + jy * 4 + p, 128, stride=24), :] = t[...].T
    for jz in range(2):
        for p in range(4):
            t = tile.at[p % 2]
            for jy in range(2):
                at = p * 4 + jy * 2 + jz
                base = 64 * jy
                t[base : base + 25, :] = up[pl.ds(at, 25, stride=16), :]
                along_z = up[pl.ds(400 + at, 25, stride=16), :]
                if jz == 1:
                    along_z = jnp.where(last_z == 1, 0.0, along_z)
                t[base + 25 : base + 50, :] = along_z
                code = jnp.broadcast_to(codes[at : at + 1, :], (5, 128))
                removed = ((code == 1) & (component >= 1) & (component <= 3)) | (
                    (code == 2) & (component == 3)
                )
                t[base + 50 : base + 55, :] = jnp.where(
                    removed, 0.0, rhs[pl.ds(at, 5, stride=16), :]
                )
                t[base + 55 : base + 64, :] = jnp.full((9, 128), vol[jy, jz], F32)
            out[pl.ds(16 + jz * 4 + p, 128, stride=24), :] = t[...].T


def column(ref, d, base, j):
    return ref[pl.ds(ROWS * d + base + j, 8, stride=5), :]


def matmul(left, right):
    return [
        [tree([left[o][i] * right[i][j] for i in range(5)]) for j in range(5)] for o in range(5)
    ]


def turned(block, by):
    return [[pltpu.roll(v, by, 1) for v in line] for line in block]


def main_kernel(
    meta, q0, q1, q2, q3, out, df, du, tf, tu, tmp, al, au, g, vv, f1, c1, change, full, sem
):
    core = meta[0]
    side = meta[1]
    copies = []
    for n, (q, dc, dx) in enumerate(((q0, 0, 0), (q1, 1, 0), (q2, 0, 1), (q3, 1, 1))):
        c = core + dc - 2 * core * dc
        x = side + dx - 2 * side * dx
        for part in range(3):
            src = q.at[:, :, pl.ds(8 * part, 8), :]
            dst = (
                df.at[:, c, part, pl.ds(0, 16), x] if part < 2 else du.at[:, c, pl.ds(0, 16), x]
            )
            copies.append(pltpu.make_async_copy(src, dst, sem.at[n * 3 + part]))
    for copy in copies:
        copy.start()
    for copy in copies:
        copy.wait()
    fl = df.reshape(32 * PITCH, 128)
    ul = du.reshape(16 * PITCH, 128)
    lane = lax.broadcasted_iota(jnp.int32, (8, 128), 1)
    sub = lax.broadcasted_iota(jnp.int32, (8, 128), 0)
    z = lane & 31
    even_z = (lane & 1) == 0

    def turn_f(d, carry):
        block = jnp.concatenate(
            [fl[pl.ds(4 * d + p, 32, stride=PITCH - 4), :] for p in range(4)], axis=0
        )
        tf[pl.ds(ROWS * d, 128), :] = block.T
        return carry

    lax.fori_loop(0, DIAGS, turn_f, 0, unroll=5)

    def turn_u(n, carry):
        for k in range(4):
            e = 4 * n + k
            for p in range(4):
                for jz in range(2):
                    tmp[k, pl.ds(p * 32 + jz, 16, stride=2), :] = ul[
                        pl.ds(8 * e + jz * 4 + p, 16, stride=PITCH - 8), :
                    ]
            tu[pl.ds(pl.multiple_of(128 * e + 128, 128), 128), :] = tmp[k].T
        return carry

    lax.fori_loop(0, 12, turn_u, 0)

    def lower_rows(k, r):
        return tf[pl.ds(ROWS * 8 * k + r, 8, stride=ROWS), :]

    def upper_rows(k, r):
        even = tu[pl.ds(64 * 8 * k + 128 + r, 8, stride=64), :]
        odd = tu[pl.ds(64 * 8 * k + 64 + r, 8, stride=64), :]
        return jnp.where(even_z, even, odd)

    def invert(k, slot):
        piv, before, after = (
            [[lower_rows(k, 25 * n + 5 * o + i) for i in range(5)] for o in range(5)]
            for n in range(3)
        )
        back = matmul(piv, before)
        ahead = matmul(piv, after)
        w = [piv]
        for _ in range(3):
            w.append([[-v for v in line] for line in matmul(back, turned(w[-1], 32))])
        inverse = {3: w[3]}
        for s in (2, 1, 0, -1, -2, -3):
            below = matmul(ahead, turned(inverse[s + 1], 96))
            inverse[s] = [
                [(w[s][o][j] - below[o][j]) if s >= 0 else -below[o][j] for j in range(5)]
                for o in range(5)
            ]
        for s in range(4):
            for o in range(5):
                for i in range(5):
                    v = inverse[s][o][i]
                    if s > 0:
                        v = v + inverse[s - 4][o][i]
                    full[slot, s * 25 + o * 5 + i] = v

    def couple(k, slot):
        totals = [[] for _ in range(5)]
        for s in range(4):
            inverse = [[full[slot, s * 25 + o * 5 + i] for i in range(5)] for o in range(5)]

            def moved(v, s=s):
                return v if s == 0 else pltpu.roll(v, 32 * s, 1)

            for n, (dest, rows, base) in enumerate(
                (
                    (al, lower_rows, 75),
                    (al, lower_rows, 100),
                    (au, upper_rows, 0),
                    (au, upper_rows, 25),
                )
            ):
                for j in range(5):
                    terms = [moved(rows(k, base + 5 * i + j)) for i in range(5)]
                    at = WIDTH * 8 * k + 8 * (s * 10 + 5 * (n % 2) + j)
                    for o in range(5):
                        dest[pl.ds(at + o, 8, stride=WIDTH), :] = tree(
                            [inverse[o][i] * terms[i] for i in range(5)]
                        )
            terms = [moved(upper_rows(k, 50 + i)) for i in range(5)]
            for o in range(5):
                totals[o].append(tree([inverse[o][i] * terms[i] for i in range(5)]))
        for o in range(5):
            g[pl.ds(64 * k + o, 8, stride=8), :] = tree(totals[o])
        vv[pl.ds(pl.multiple_of(8 * k, 8), 8), :] = upper_rows(k, 55)

    invert(0, 0)

    def prepare(k, carry):
        couple(k - 1, (k - 1) % 2)
        invert(k, k % 2)
        return carry

    lax.fori_loop(1, 12, prepare, 0)
    couple(11, 1)

    def product(ref, d, f, step):
        terms = []
        start = WIDTH * d
        for s in range(4):
            by_y = f if s == 0 else pltpu.roll(f, 32 * s, 1)
            by_z = pltpu.roll(f, (32 * s + step) % 128, 1)
            for i in range(5):
                terms.append(ref[pl.ds(start + 8 * (s * 10 + i), 8), :] * spread(by_y, i))
            for i in range(5):
                terms.append(ref[pl.ds(start + 8 * (s * 10 + 5 + i), 8), :] * spread(by_z, i))
        return tree(terms)

    def tile(d):
        return pl.ds(pl.multiple_of(8 * d, 8), 8)

    def inside(d):
        return (z <= d) & (z >= d - (NY - 1))

    nothing = jnp.zeros((8, 128), F32)

    def forward_first(d, f):
        f = jnp.where(inside(d), g[tile(d), :] - product(al, d, f, 1), 0.0)
        f1[d] = f
        return f

    lax.fori_loop(0, DIAGS, forward_first, nothing)

    def backward_first(n, f):
        d = DIAGS - 1 - n
        coupled = product(au, d, f, -1)
        f = jnp.where(inside(d), f1[d] - coupled, 0.0)
        f1[d] = f
        g[tile(d), :] = coupled
        return f

    lax.fori_loop(0, DIAGS, backward_first, nothing)

    def forward_second(d, f):
        coupled = product(al, d, f, 1)
        f = jnp.where(inside(d), -(g[tile(d), :] + coupled), 0.0)
        c1[d] = coupled
        return f

    lax.fori_loop(0, DIAGS, forward_second, nothing)

    def backward_second(n, f):
        d = DIAGS - 1 - n
        coupled = product(au, d, f, -1)
        f = jnp.where(inside(d), -(c1[d] + coupled), 0.0)
        f1[d] = f1[d] + f
        change[tile(d + 1), :] = jnp.where(inside(d), coupled, 0.0)
        return f

    change[0:8, :] = nothing
    lax.fori_loop(0, DIAGS, backward_second, nothing)

    def residual(d, carry):
        before = change[tile(d), :]
        by_z = pltpu.roll(before, 1, 1)
        g[tile(d), :] = vv[pl.ds(d, 1), :] * tree(
            [column(tf, d, 75, i) * spread(before, i) for i in range(5)]
            + [column(tf, d, 100, i) * spread(by_z, i) for i in range(5)]
        )
        return carry

    lax.fori_loop(0, DIAGS, residual, 0, unroll=5)
    for bit, length in ((16, 79), (8, 71), (4, 67), (2, 65), (1, 64)):
        far = (z & bit) != 0
        for d in range(length):
            f1[d] = jnp.where(far, f1[d + bit], f1[d])
            here, there = pl.ds(8 * d, 8), pl.ds(8 * (d + bit), 8)
            g[here, :] = jnp.where(far, g[there, :], g[here, :])

    owner_y = lane & 15
    owner_z = lane >> 4

    def collect(n, sums):
        sums = list(sums)
        for jy in range(2):
            y = 4 * n + 2 * side + jy
            value = f1[y]
            total = g[tile(y), :]
            for by in (16, 8, 4, 2, 1):
                total = total + pltpu.roll(total, 128 - by, 1)
            for jz in range(2):
                merged = jnp.where(sub < 5, value, pltpu.roll(total, 5 if jz == 0 else 2, 0))
                for p in range(4):
                    index = jnp.where(sub < 5, p * 32 + 4 * owner_z + 2 * core + jz, p * 32)
                    picked = jnp.take_along_axis(merged, index, axis=1)
                    k = p * 4 + jz * 2 + jy
                    sums[k] = jnp.where(owner_y == n, picked, sums[k])
        return tuple(sums)

    slots = lax.fori_loop(0, 16, collect, (nothing,) * 16, unroll=4)
    out[...] = jnp.concatenate(slots, axis=0).T


def unpack_kernel(meta, slots, correction, coarse):
    values = slots[...].T
    gz = meta[4]
    for p in range(4):
        for jy in range(2):
            for jz in range(2):
                k = 8 * (p * 4 + jz * 2 + jy)
                correction[pl.ds(p * 4 + jy * 2 + jz, 5, stride=16), :] = values[k : k + 5]
                extra = pltpu.roll(values[k : k + 8], (128 - 8 * gz) % 128, 1)
                if jz == 0:
                    coarse[pl.ds(p * 2 + jy, 3, stride=8), :] = extra[5:8]
                else:
                    coarse[pl.ds(24 + p * 2 + jy, 2, stride=8), :] = extra[5:7]


def on_device(rhs, codes, piv, low_x, up_x, low, up, volume):
    core = lax.axis_index("c")
    side = lax.axis_index("xl")
    gz = lax.axis_index("z") * 2 + core
    meta = jnp.stack(
        [core, side, (gz == 0).astype(jnp.int32), (gz == 15).astype(jnp.int32), gz]
    ).astype(jnp.int32)
    smem = pl.BlockSpec(memory_space=SMEM)
    vmem = pl.BlockSpec(memory_space=VMEM)
    hbm = pl.BlockSpec(memory_space=pl.ANY)
    packed = pl.pallas_call(
        pack_kernel,
        out_shape=jax.ShapeDtypeStruct((128 * 24, 128), F32),
        in_specs=[smem, smem] + [vmem] * 7,
        out_specs=vmem,
        scratch_shapes=[pltpu.VMEM((2, 128, 128), F32)],
        compiler_params=pltpu.CompilerParams(vmem_limit_bytes=32 << 20),
        name="pack",
    )(
        meta,
        volume,
        rhs.reshape(80, 128),
        codes.reshape(16, 128),
        piv.reshape(400, 128),
        low_x.reshape(300, 128),
        up_x.reshape(300, 128),
        low.reshape(800, 128),
        up.reshape(800, 128),
    )
    mine = lax.all_to_all(packed.reshape(128, 24, 128), GROUP, 0, 0, tiled=True)
    other_x = lax.ppermute(mine, "xl", SWAP)
    other_c = lax.ppermute(mine, "c", SWAP)
    other_cx = lax.ppermute(other_x, "c", SWAP)
    quarters = [v.reshape(8, 16, 24, 128) for v in (mine, other_c, other_x, other_cx)]
    diag = pltpu.VMEM((96, 8, 128), F32)
    slots = pl.pallas_call(
        main_kernel,
        out_shape=jax.ShapeDtypeStruct((128, 128), F32),
        in_specs=[smem] + [hbm] * 4,
        out_specs=vmem,
        scratch_shapes=[
            pltpu.VMEM((8, 2, 2, 17, 2, 8, 128), F32),
            pltpu.VMEM((8, 2, 17, 2, 8, 128), F32),
            pltpu.VMEM((96 * ROWS, 128), F32),
            pltpu.VMEM((50 * 128, 128), F32),
            pltpu.VMEM((4, 128, 128), F32),
            pltpu.VMEM((96 * WIDTH, 128), F32),
            pltpu.VMEM((96 * WIDTH, 128), F32),
            pltpu.VMEM((96 * 8, 128), F32),
            pltpu.VMEM((96, 128), F32),
            diag,
            diag,
            pltpu.VMEM((97 * 8, 128), F32),
            pltpu.VMEM((2, 100, 8, 128), F32),
            pltpu.SemaphoreType.DMA((12,)),
        ],
        compiler_params=pltpu.CompilerParams(vmem_limit_bytes=60 << 20),
        name="sweeps",
    )(meta, *quarters)
    slots = lax.all_to_all(slots.reshape(128, 1, 128), GROUP, 0, 0, tiled=True)
    correction, coarse = pl.pallas_call(
        unpack_kernel,
        out_shape=(
            jax.ShapeDtypeStruct((80, 128), F32),
            jax.ShapeDtypeStruct((40, 128), F32),
        ),
        in_specs=[smem, vmem],
        out_specs=(vmem, vmem),
        name="unpack",
    )(meta, slots.reshape(128, 128))
    return correction.reshape(5, 4, 2, 2, 128), coarse[:, :8].reshape(5, 4, 2, 8)


def solution(mesh):
    split = Mesh(mesh.devices.reshape(8, 2, 2, 8, 2), ("cy", "xh", "xl", "z", "c"))
    gy = ("cy", "xh", "xl")
    gz = ("z", "c")
    return jax.shard_map(
        on_device,
        mesh=split,
        in_specs=(
            P(None, None, gy, gz, None),
            P(None, gy, gz, None),
            P(None, None, None, gy, gz, None),
            P(None, None, None, gy, gz, None),
            P(None, None, None, gy, gz, None),
            P(None, None, None, None, gy, gz, None),
            P(None, None, None, None, gy, gz, None),
            P(gy, gz),
        ),
        out_specs=(P(None, None, gy, gz, None), P(None, None, gy, gz)),
        check_vma=False,
    )
```

```python
from itertools import chain

import jax
import jax.numpy as jnp
from jax import lax
from jax.experimental import pallas as pl
from jax.experimental.pallas import tpu as pltpu
from jax.sharding import Mesh, PartitionSpec as P

F32 = jnp.float32
NZ = 32
NY = 64
DIAGS = NY + NZ - 1
PITCH = 272
ROWS = 145
WIDTH = 321
SHARE = 13
SWAP = [(0, 1), (1, 0)]
GROUP = ("z", "cy", "xh")
SMEM = pltpu.SMEM
VMEM = pltpu.VMEM


def tree(terms):
    terms = list(terms)
    while len(terms) > 1:
        terms = [
            terms[k] + terms[k + 1] if k + 1 < len(terms) else terms[k]
            for k in range(0, len(terms), 2)
        ]
    return terms[0]


def spread(value, i):
    return jnp.broadcast_to(value[i : i + 1, :], (8, 128))


def pack_kernel(
    meta, vol, rhs_in, codes_in, piv_in, low_x_in, up_x_in, low_in, up_in, out,
    rhs, codes, piv, low_x, up_x, low, up, tile, sem,
):
    copies = [
        pltpu.make_async_copy(src, dst, sem.at[n])
        for n, (src, dst) in enumerate(
            (
                (piv_in, piv),
                (low_x_in, low_x),
                (up_x_in, up_x),
                (low_in, low),
                (up_in, up),
                (rhs_in, rhs),
                (codes_in, codes),
            )
        )
    ]
    for copy in copies:
        copy.start()
    for copy in copies:
        copy.wait()
    first_z = meta[2]
    last_z = meta[3]
    zero = jnp.zeros((25, 128), F32)
    component = lax.broadcasted_iota(jnp.int32, (5, 128), 0)
    for jz in range(2):
        for jy in range(2):
            for p in range(4):
                at = p * 4 + jy * 2 + jz
                t = tile.at[(jy * 4 + p) % 2]
                t[0:25, :] = piv[pl.ds(at, 25, stride=16), :]
                t[25:50, :] = low_x[pl.ds(2 * p - 2 + jy, 25, stride=6), jz, :] if p > 0 else zero
                t[50:75, :] = up_x[pl.ds(2 * p + jy, 25, stride=6), jz, :] if p < 3 else zero
                t[75:100, :] = low[pl.ds(at, 25, stride=16), :]
                along_z = low[pl.ds(400 + at, 25, stride=16), :]
                if jz == 0:
                    along_z = jnp.where(first_z == 1, 0.0, along_z)
                t[100:125, :] = along_z
                t[125:128, :] = zero[:3]
                out[pl.ds(jz * 8 + jy * 4 + p, 128, stride=24), :] = t[...].T
    for jz in range(2):
        for p in range(4):
            t = tile.at[p % 2]
            for jy in range(2):
                at = p * 4 + jy * 2 + jz
                base = 64 * jy
                t[base : base + 25, :] = up[pl.ds(at, 25, stride=16), :]
                along_z = up[pl.ds(400 + at, 25, stride=16), :]
                if jz == 1:
                    along_z = jnp.where(last_z == 1, 0.0, along_z)
                t[base + 25 : base + 50, :] = along_z
                code = jnp.broadcast_to(codes[at : at + 1, :], (5, 128))
                removed = ((code == 1) & (component >= 1) & (component <= 3)) | (
                    (code == 2) & (component == 3)
                )
                t[base + 50 : base + 55, :] = jnp.where(
                    removed, 0.0, rhs[pl.ds(at, 5, stride=16), :]
                )
                t[base + 55 : base + 64, :] = jnp.full((9, 128), vol[jy, jz], F32)
            out[pl.ds(16 + jz * 4 + p, 128, stride=24), :] = t[...].T


def column(ref, d, base, j):
    return ref[pl.ds(ROWS * d + base + j, 8, stride=5), :]


def matmul(left, right, into):
    for o in range(5):
        into.append([tree([left[o][i] * right[i][j] for i in range(5)]) for j in range(5)])
        yield


def mixed(*works):
    works = list(works)
    while works:
        for work in list(works):
            try:
                next(work)
            except StopIteration:
                works.remove(work)
                continue
            yield


def turned(block, by):
    return [[pltpu.roll(v, by, 1) for v in line] for line in block]


def main_kernel(
    meta, q0, q1, q2, q3, out, df, du, tf, tu, tmp, al0, al1, au0, au1, g0, g1, h, vv, f1, c1, change, full0, full1, sem
):
    core = meta[0]
    side = meta[1]
    copies = []
    for n, (q, dc, dx) in enumerate(((q0, 0, 0), (q1, 1, 0), (q2, 0, 1), (q3, 1, 1))):
        c = core + dc - 2 * core * dc
        x = side + dx - 2 * side * dx
        for part in range(3):
            src = q.at[:, :, pl.ds(8 * part, 8), :]
            dst = (
                df.at[:, c, part, pl.ds(0, 16), x] if part < 2 else du.at[:, c, pl.ds(0, 16), x]
            )
            copies.append(pltpu.make_async_copy(src, dst, sem.at[n * 3 + part]))
    for copy in copies:
        copy.start()
    for copy in copies:
        copy.wait()
    fl = df.reshape(32 * PITCH, 128)
    ul = du.reshape(16 * PITCH, 128)
    lane = lax.broadcasted_iota(jnp.int32, (8, 128), 1)
    sub = lax.broadcasted_iota(jnp.int32, (8, 128), 0)
    z = lane & 31
    even_z = (lane & 1) == 0

    def turn_f(d, carry):
        block = jnp.concatenate(
            [fl[pl.ds(4 * d + p, 32, stride=PITCH - 4), :] for p in range(4)], axis=0
        )
        tf[pl.ds(ROWS * d, 128), :] = block.T
        return carry

    lax.fori_loop(0, DIAGS, turn_f, 0, unroll=5)

    def turn_u(n, carry):
        for k in range(4):
            e = 4 * n + k
            for p in range(4):
                for jz in range(2):
                    tmp[k, pl.ds(p * 32 + jz, 16, stride=2), :] = ul[
                        pl.ds(8 * e + jz * 4 + p, 16, stride=PITCH - 8), :
                    ]
            tu[pl.ds(pl.multiple_of(128 * e + 128, 128), 128), :] = tmp[k].T
        return carry

    lax.fori_loop(0, 12, turn_u, 0)

    def lower_rows(k, r):
        return tf[pl.ds(ROWS * 8 * k + r, 8, stride=ROWS), :]

    def upper_rows(k, r):
        even = tu[pl.ds(64 * 8 * k + 128 + r, 8, stride=64), :]
        odd = tu[pl.ds(64 * 8 * k + 64 + r, 8, stride=64), :]
        return jnp.where(even_z, even, odd)

    al, au, g, full = (al0, al1), (au0, au1), (g0, g1), (full0, full1)

    def invert(n, half):
        k = 2 * n + half
        piv, before, after = (
            [[lower_rows(k, 25 * m + 5 * o + i) for i in range(5)] for o in range(5)]
            for m in range(3)
        )
        back, ahead = [], []
        yield from matmul(piv, before, back)
        yield from matmul(piv, after, ahead)
        w = [piv]
        for _ in range(3):
            product_now = []
            yield from matmul(back, turned(w[-1], 32), product_now)
            w.append([[-v for v in line] for line in product_now])
        inverse = {3: w[3]}
        for s in (2, 1, 0, -1, -2, -3):
            below = []
            yield from matmul(ahead, turned(inverse[s + 1], 96), below)
            inverse[s] = [
                [(w[s][o][j] - below[o][j]) if s >= 0 else -below[o][j] for j in range(5)]
                for o in range(5)
            ]
        for s in range(4):
            for o in range(5):
                for i in range(5):
                    v = inverse[s][o][i]
                    if s > 0:
                        v = v + inverse[s - 4][o][i]
                    full[half][n, s * 25 + o * 5 + i] = v

    def couple(n, half, dest, rows, base):
        k = 2 * n + half
        for s in range(4):
            inverse = [[full[half][n, s * 25 + o * 5 + i] for i in range(5)] for o in range(5)]
            for m in range(2):
                for j in range(5):
                    terms = [rows(k, base + 25 * m + 5 * i + j) for i in range(5)]
                    if s > 0:
                        terms = [pltpu.roll(v, 32 * s, 1) for v in terms]
                    at = WIDTH * 8 * n + 8 * (s * 10 + 5 * m + j)
                    for o in range(5):
                        dest[half][pl.ds(at + o, 8, stride=WIDTH), :] = tree(
                            [inverse[o][i] * terms[i] for i in range(5)]
                        )
                    yield

    def couple_lower(n, half):
        return couple(n, half, al, lower_rows, 75)

    def couple_upper(n, half):
        return couple(n, half, au, upper_rows, 0)

    def start_values(n, half):
        k = 2 * n + half
        totals = [[] for _ in range(5)]
        for s in range(4):
            terms = [upper_rows(k, 50 + i) for i in range(5)]
            if s > 0:
                terms = [pltpu.roll(v, 32 * s, 1) for v in terms]
            for o in range(5):
                totals[o].append(
                    tree([full[half][n, s * 25 + o * 5 + i] * terms[i] for i in range(5)])
                )
            yield
        for o in range(5):
            g[half][pl.ds(64 * n + o, 8, stride=8), :] = tree(totals[o])
        vv[pl.ds(pl.multiple_of(8 * k, 8), 8), :] = upper_rows(k, 55)

    def product(ref, start, f, step):
        terms = []
        for s in range(4):
            by_y = f if s == 0 else pltpu.roll(f, 32 * s, 1)
            by_z = pltpu.roll(f, (32 * s + step) % 128, 1)
            for i in range(5):
                terms.append(ref[pl.ds(start + 8 * (s * 10 + i), 8), :] * spread(by_y, i))
            for i in range(5):
                terms.append(ref[pl.ds(start + 8 * (s * 10 + 5 + i), 8), :] * spread(by_z, i))
        return tree(terms)

    def tile(d):
        return pl.ds(pl.multiple_of(8 * d, 8), 8)

    def inside(d):
        return (z <= d) & (z >= d - (NY - 1))

    nothing = jnp.zeros((8, 128), F32)

    def finish(work):
        for _ in work:
            pass

    def sweep(n, half, f, step, update, work=(), share=0):
        work = iter(work)
        for m in range(8):
            e = m if step == 1 else 7 - m
            d = 16 * n + 8 * half + e
            matrix = (al if step == 1 else au)[half]
            coupled = product(matrix, WIDTH * (8 * n + e), f, step)
            f = update(n, half, e, d, coupled)
            for _ in range(share):
                next(work, None)
        finish(work)
        return f

    def forward_first(n, half, e, d, coupled):
        f = jnp.where(inside(d), g[half][pl.ds(64 * n + 8 * e, 8), :] - coupled, 0.0)
        f1[d] = f
        return f

    def backward_first(n, half, e, d, coupled):
        f = jnp.where(inside(d), f1[d] - coupled, 0.0)
        f1[d] = f
        h[tile(d), :] = coupled
        return f

    def forward_second(n, half, e, d, coupled):
        f = jnp.where(inside(d), -(h[tile(d), :] + coupled), 0.0)
        c1[d] = coupled
        return f

    def backward_second(n, half, e, d, coupled):
        f = jnp.where(inside(d), -(c1[d] + coupled), 0.0)
        f1[d] = f1[d] + f
        change[tile(d + 1), :] = jnp.where(inside(d), coupled, 0.0)
        return f

    finish(invert(0, 0))
    finish(couple_lower(0, 0))
    finish(start_values(0, 0))
    finish(invert(0, 1))

    def first_rows(n, f):
        f = sweep(
            n, 0, f, 1, forward_first,
            chain(mixed(couple_lower(n, 1), invert(n + 1, 0)), start_values(n, 1)), SHARE,
        )
        return sweep(
            n, 1, f, 1, forward_first,
            chain(mixed(couple_lower(n + 1, 0), invert(n + 1, 1)), start_values(n + 1, 0)), SHARE,
        )

    f = lax.fori_loop(0, 5, first_rows, nothing)
    f = sweep(5, 0, f, 1, forward_first, chain(couple_lower(5, 1), start_values(5, 1)), 6)
    sweep(5, 1, f, 1, forward_first, couple_upper(5, 1), 6)

    def last_rows(m, f):
        n = 5 - m
        f = sweep(n, 1, f, -1, backward_first, couple_upper(n, 0), 6)
        return sweep(n, 0, f, -1, backward_first, couple_upper(n - 1, 1), 6)

    f = lax.fori_loop(0, 5, last_rows, nothing)
    f = sweep(0, 1, f, -1, backward_first, couple_upper(0, 0), 6)
    sweep(0, 0, f, -1, backward_first)

    def again_forward(n, f):
        return sweep(n, 1, sweep(n, 0, f, 1, forward_second), 1, forward_second)

    lax.fori_loop(0, 6, again_forward, nothing)
    change[0:8, :] = nothing

    def again_backward(m, f):
        n = 5 - m
        return sweep(n, 0, sweep(n, 1, f, -1, backward_second), -1, backward_second)

    lax.fori_loop(0, 6, again_backward, nothing)

    def residual(d, carry):
        before = change[tile(d), :]
        by_z = pltpu.roll(before, 1, 1)
        h[tile(d), :] = vv[pl.ds(d, 1), :] * tree(
            [column(tf, d, 75, i) * spread(before, i) for i in range(5)]
            + [column(tf, d, 100, i) * spread(by_z, i) for i in range(5)]
        )
        return carry

    lax.fori_loop(0, DIAGS, residual, 0, unroll=5)
    for bit, length in ((16, 79), (8, 71), (4, 67), (2, 65), (1, 64)):
        far = (z & bit) != 0
        for d in range(length):
            f1[d] = jnp.where(far, f1[d + bit], f1[d])
            here, there = pl.ds(8 * d, 8), pl.ds(8 * (d + bit), 8)
            h[here, :] = jnp.where(far, h[there, :], h[here, :])

    owner_y = lane & 15
    owner_z = lane >> 4

    def collect(n, sums):
        sums = list(sums)
        for jy in range(2):
            y = 4 * n + 2 * side + jy
            value = f1[y]
            total = h[tile(y), :]
            for by in (16, 8, 4, 2, 1):
                total = total + pltpu.roll(total, 128 - by, 1)
            for jz in range(2):
                merged = jnp.where(sub < 5, value, pltpu.roll(total, 5 if jz == 0 else 2, 0))
                for p in range(4):
                    index = jnp.where(sub < 5, p * 32 + 4 * owner_z + 2 * core + jz, p * 32)
                    picked = jnp.take_along_axis(merged, index, axis=1)
                    k = p * 4 + jz * 2 + jy
                    sums[k] = jnp.where(owner_y == n, picked, sums[k])
        return tuple(sums)

    slots = lax.fori_loop(0, 16, collect, (nothing,) * 16, unroll=4)
    out[...] = jnp.concatenate(slots, axis=0).T


def unpack_kernel(meta, slots, correction, coarse):
    values = slots[...].T
    gz = meta[4]
    for p in range(4):
        for jy in range(2):
            for jz in range(2):
                k = 8 * (p * 4 + jz * 2 + jy)
                correction[pl.ds(p * 4 + jy * 2 + jz, 5, stride=16), :] = values[k : k + 5]
                extra = pltpu.roll(values[k : k + 8], (128 - 8 * gz) % 128, 1)
                if jz == 0:
                    coarse[pl.ds(p * 2 + jy, 3, stride=8), :] = extra[5:8]
                else:
                    coarse[pl.ds(24 + p * 2 + jy, 2, stride=8), :] = extra[5:7]


def on_device(rhs, codes, piv, low_x, up_x, low, up, volume):
    core = lax.axis_index("c")
    side = lax.axis_index("xl")
    gz = lax.axis_index("z") * 2 + core
    meta = jnp.stack(
        [core, side, (gz == 0).astype(jnp.int32), (gz == 15).astype(jnp.int32), gz]
    ).astype(jnp.int32)
    smem = pl.BlockSpec(memory_space=SMEM)
    vmem = pl.BlockSpec(memory_space=VMEM)
    hbm = pl.BlockSpec(memory_space=pl.ANY)
    packed = pl.pallas_call(
        pack_kernel,
        out_shape=jax.ShapeDtypeStruct((128 * 24, 128), F32),
        in_specs=[smem, smem] + [hbm] * 7,
        out_specs=vmem,
        scratch_shapes=[
            pltpu.VMEM((80, 128), F32),
            pltpu.VMEM((16, 128), jnp.int32),
            pltpu.VMEM((400, 128), F32),
            pltpu.VMEM((150, 2, 128), F32),
            pltpu.VMEM((150, 2, 128), F32),
            pltpu.VMEM((800, 128), F32),
            pltpu.VMEM((800, 128), F32),
            pltpu.VMEM((2, 128, 128), F32),
            pltpu.SemaphoreType.DMA((7,)),
        ],
        compiler_params=pltpu.CompilerParams(vmem_limit_bytes=60 << 20),
        name="pack",
    )(
        meta,
        volume,
        rhs.reshape(80, 128),
        codes.reshape(16, 128),
        piv.reshape(400, 128),
        low_x.reshape(150, 2, 128),
        up_x.reshape(150, 2, 128),
        low.reshape(800, 128),
        up.reshape(800, 128),
    )
    mine = lax.all_to_all(packed.reshape(128, 24, 128), GROUP, 0, 0, tiled=True)
    other_x = lax.ppermute(mine, "xl", SWAP)
    other_c = lax.ppermute(mine, "c", SWAP)
    other_cx = lax.ppermute(other_x, "c", SWAP)
    quarters = [v.reshape(8, 16, 24, 128) for v in (mine, other_c, other_x, other_cx)]
    diag = pltpu.VMEM((96, 8, 128), F32)
    slots = pl.pallas_call(
        main_kernel,
        out_shape=jax.ShapeDtypeStruct((128, 128), F32),
        in_specs=[smem] + [hbm] * 4,
        out_specs=vmem,
        scratch_shapes=[
            pltpu.VMEM((8, 2, 2, 17, 2, 8, 128), F32),
            pltpu.VMEM((8, 2, 17, 2, 8, 128), F32),
            pltpu.VMEM((96 * ROWS, 128), F32),
            pltpu.VMEM((50 * 128, 128), F32),
            pltpu.VMEM((4, 128, 128), F32),
            *[pltpu.VMEM((48 * WIDTH, 128), F32)] * 4,
            pltpu.VMEM((48 * 8, 128), F32),
            pltpu.VMEM((48 * 8, 128), F32),
            pltpu.VMEM((96 * 8, 128), F32),
            pltpu.VMEM((96, 128), F32),
            diag,
            diag,
            pltpu.VMEM((97 * 8, 128), F32),
            pltpu.VMEM((6, 100, 8, 128), F32),
            pltpu.VMEM((6, 100, 8, 128), F32),
            pltpu.SemaphoreType.DMA((12,)),
        ],
        compiler_params=pltpu.CompilerParams(vmem_limit_bytes=60 << 20),
        name="sweeps",
    )(meta, *quarters)
    slots = lax.all_to_all(slots.reshape(128, 1, 128), GROUP, 0, 0, tiled=True)
    correction, coarse = pl.pallas_call(
        unpack_kernel,
        out_shape=(
            jax.ShapeDtypeStruct((80, 128), F32),
            jax.ShapeDtypeStruct((40, 128), F32),
        ),
        in_specs=[smem, vmem],
        out_specs=(vmem, vmem),
        name="unpack",
    )(meta, slots.reshape(128, 128))
    return correction.reshape(5, 4, 2, 2, 128), coarse[:, :8].reshape(5, 4, 2, 8)


def solution(mesh):
    split = Mesh(mesh.devices.reshape(8, 2, 2, 8, 2), ("cy", "xh", "xl", "z", "c"))
    gy = ("cy", "xh", "xl")
    gz = ("z", "c")
    return jax.shard_map(
        on_device,
        mesh=split,
        in_specs=(
            P(None, None, gy, gz, None),
            P(None, gy, gz, None),
            P(None, None, None, gy, gz, None),
            P(None, None, None, gy, gz, None),
            P(None, None, None, gy, gz, None),
            P(None, None, None, None, gy, gz, None),
            P(None, None, None, None, gy, gz, None),
            P(gy, gz),
        ),
        out_specs=(P(None, None, gy, gz, None), P(None, None, gy, gz)),
        check_vma=False,
    )
```

```python
from itertools import chain

import jax
import jax.numpy as jnp
from jax import lax
from jax.experimental import pallas as pl
from jax.experimental.pallas import tpu as pltpu
from jax.sharding import Mesh, PartitionSpec as P

F32 = jnp.float32
NZ = 32
NY = 64
DIAGS = NY + NZ - 1
PITCH = 272
ROWS = 145
WIDTH = 321
SHARE = 13
SWAP = [(0, 1), (1, 0)]
GROUP = ("z", "cy", "xh")
SMEM = pltpu.SMEM
VMEM = pltpu.VMEM


def tree(terms):
    terms = list(terms)
    while len(terms) > 1:
        terms = [
            terms[k] + terms[k + 1] if k + 1 < len(terms) else terms[k]
            for k in range(0, len(terms), 2)
        ]
    return terms[0]


def spread(value, i):
    return jnp.broadcast_to(value[i : i + 1, :], (8, 128))


def pack_kernel(
    vol, rhs_in, codes_in, piv_in, low_x_in, up_x_in, low_in, up_in, out,
    rhs, codes, piv, low_x, up_x, low, up, tile, sem,
):
    copies = [
        pltpu.make_async_copy(src, dst, sem.at[n])
        for n, (src, dst) in enumerate(
            (
                (piv_in, piv),
                (low_x_in, low_x),
                (up_x_in, up_x),
                (low_in, low),
                (up_in, up),
                (rhs_in, rhs),
                (codes_in, codes),
            )
        )
    ]
    for copy in copies:
        copy.start()
    for copy in copies[:4]:
        copy.wait()
    gz = lax.axis_index("z") * 2 + lax.axis_index("c")
    zero = jnp.zeros((25, 128), F32)
    component = lax.broadcasted_iota(jnp.int32, (5, 128), 0)
    for jz in range(2):
        for jy in range(2):
            for p in range(4):
                at = p * 4 + jy * 2 + jz
                t = tile.at[(jy * 4 + p) % 2]
                t[0:25, :] = piv[pl.ds(at, 25, stride=16), :]
                t[25:50, :] = low_x[pl.ds(2 * p - 2 + jy, 25, stride=6), jz, :] if p > 0 else zero
                t[50:75, :] = up_x[pl.ds(2 * p + jy, 25, stride=6), jz, :] if p < 3 else zero
                t[75:100, :] = low[pl.ds(at, 25, stride=16), :]
                along_z = low[pl.ds(400 + at, 25, stride=16), :]
                if jz == 0:
                    along_z = jnp.where(gz == 0, 0.0, along_z)
                t[100:125, :] = along_z
                t[125:128, :] = zero[:3]
                out[pl.ds(jz * 8 + jy * 4 + p, 128, stride=24), :] = t[...].T
    for copy in copies[4:]:
        copy.wait()
    for jz in range(2):
        for p in range(4):
            t = tile.at[p % 2]
            for jy in range(2):
                at = p * 4 + jy * 2 + jz
                base = 64 * jy
                t[base : base + 25, :] = up[pl.ds(at, 25, stride=16), :]
                along_z = up[pl.ds(400 + at, 25, stride=16), :]
                if jz == 1:
                    along_z = jnp.where(gz == 15, 0.0, along_z)
                t[base + 25 : base + 50, :] = along_z
                code = jnp.broadcast_to(codes[at : at + 1, :], (5, 128))
                removed = ((code == 1) & (component >= 1) & (component <= 3)) | (
                    (code == 2) & (component == 3)
                )
                t[base + 50 : base + 55, :] = jnp.where(
                    removed, 0.0, rhs[pl.ds(at, 5, stride=16), :]
                )
                t[base + 55 : base + 64, :] = jnp.full((9, 128), vol[jy, jz], F32)
            out[pl.ds(16 + jz * 4 + p, 128, stride=24), :] = t[...].T


def column(ref, d, base, j):
    return ref[pl.ds(ROWS * d + base + j, 8, stride=5), :]


def matmul(left, right, into):
    for o in range(5):
        into.append([tree([left[o][i] * right[i][j] for i in range(5)]) for j in range(5)])
        yield


def mixed(*works):
    works = list(works)
    while works:
        for work in list(works):
            try:
                next(work)
            except StopIteration:
                works.remove(work)
                continue
            yield


def turned(block, by):
    return [[pltpu.roll(v, by, 1) for v in line] for line in block]


def main_kernel(
    q0, q1, q2, q3, out, df, du, tf, tu, tmp, al0, al1, au0, au1, g0, g1, h, vv, f1, c1, full0, full1, sem
):
    core = lax.axis_index("c")
    side = lax.axis_index("xl")
    copies = []
    for n, (q, dc, dx) in enumerate(((q0, 0, 0), (q1, 1, 0), (q2, 0, 1), (q3, 1, 1))):
        c = core + dc - 2 * core * dc
        x = side + dx - 2 * side * dx
        for part in range(3):
            src = q.at[:, :, pl.ds(8 * part, 8), :]
            dst = (
                df.at[:, c, part, pl.ds(0, 16), x] if part < 2 else du.at[:, c, pl.ds(0, 16), x]
            )
            copies.append(pltpu.make_async_copy(src, dst, sem.at[n * 3 + part]))
    for copy in copies[2::3]:
        copy.start()
    for part in range(2):
        for copy in copies[part::3]:
            copy.start()
    for copy in copies[2::3]:
        copy.wait()
    fl = df.reshape(32 * PITCH, 128)
    ul = du.reshape(16 * PITCH, 128)
    lane = lax.broadcasted_iota(jnp.int32, (8, 128), 1)
    sub = lax.broadcasted_iota(jnp.int32, (8, 128), 0)
    z = lane & 31
    even_z = (lane & 1) == 0

    def turn_u(n, carry):
        for k in range(4):
            e = 4 * n + k
            for p in range(4):
                for jz in range(2):
                    tmp[k, pl.ds(p * 32 + jz, 16, stride=2), :] = ul[
                        pl.ds(8 * e + jz * 4 + p, 16, stride=PITCH - 8), :
                    ]
            tu[pl.ds(pl.multiple_of(128 * e + 128, 128), 128), :] = tmp[k].T
        return carry

    lax.fori_loop(0, 12, turn_u, 0)

    for part in range(2):
        for copy in copies[part::3]:
            copy.wait()

    def turn_f(d, carry):
        block = jnp.concatenate(
            [fl[pl.ds(4 * d + p, 32, stride=PITCH - 4), :] for p in range(4)], axis=0
        )
        tf[pl.ds(ROWS * d, 128), :] = block.T
        return carry

    lax.fori_loop(0, DIAGS, turn_f, 0, unroll=5)

    def lower_rows(k, r):
        return tf[pl.ds(ROWS * 8 * k + r, 8, stride=ROWS), :]

    def upper_rows(k, r):
        even = tu[pl.ds(64 * 8 * k + 128 + r, 8, stride=64), :]
        odd = tu[pl.ds(64 * 8 * k + 64 + r, 8, stride=64), :]
        return jnp.where(even_z, even, odd)

    al, au, g, full = (al0, al1), (au0, au1), (g0, g1), (full0, full1)

    def invert(n, half):
        k = 2 * n + half
        piv, before, after = (
            [[lower_rows(k, 25 * m + 5 * o + i) for i in range(5)] for o in range(5)]
            for m in range(3)
        )
        back, ahead = [], []
        yield from matmul(piv, before, back)
        yield from matmul(piv, after, ahead)
        w = [piv]
        for _ in range(3):
            product_now = []
            yield from matmul(back, turned(w[-1], 32), product_now)
            w.append([[-v for v in line] for line in product_now])
        inverse = {3: w[3]}
        for s in (2, 1, 0, -1, -2, -3):
            below = []
            yield from matmul(ahead, turned(inverse[s + 1], 96), below)
            inverse[s] = [
                [(w[s][o][j] - below[o][j]) if s >= 0 else -below[o][j] for j in range(5)]
                for o in range(5)
            ]
        for s in range(4):
            for o in range(5):
                for i in range(5):
                    v = inverse[s][o][i]
                    if s > 0:
                        v = v + inverse[s - 4][o][i]
                    full[half][n, s * 25 + o * 5 + i] = v

    def couple(n, half, dest, rows, base):
        k = 2 * n + half
        for s in range(4):
            inverse = [[full[half][n, s * 25 + o * 5 + i] for i in range(5)] for o in range(5)]
            for m in range(2):
                for j in range(5):
                    terms = [rows(k, base + 25 * m + 5 * i + j) for i in range(5)]
                    if s > 0:
                        terms = [pltpu.roll(v, 32 * s, 1) for v in terms]
                    at = WIDTH * 8 * n + 8 * (s * 10 + 5 * m + j)
                    for o in range(5):
                        dest[half][pl.ds(at + o, 8, stride=WIDTH), :] = tree(
                            [inverse[o][i] * terms[i] for i in range(5)]
                        )
                    yield

    def couple_lower(n, half):
        return couple(n, half, al, lower_rows, 75)

    def couple_upper(n, half):
        return couple(n, half, au, upper_rows, 0)

    def start_values(n, half):
        k = 2 * n + half
        totals = [[] for _ in range(5)]
        for s in range(4):
            terms = [upper_rows(k, 50 + i) for i in range(5)]
            if s > 0:
                terms = [pltpu.roll(v, 32 * s, 1) for v in terms]
            for o in range(5):
                totals[o].append(
                    tree([full[half][n, s * 25 + o * 5 + i] * terms[i] for i in range(5)])
                )
            yield
        for o in range(5):
            g[half][pl.ds(64 * n + o, 8, stride=8), :] = tree(totals[o])
        vv[pl.ds(pl.multiple_of(8 * k, 8), 8), :] = upper_rows(k, 55)

    def product(ref, start, f, step):
        sums = []
        for s in range(4):
            for m, by in enumerate((32 * s, (32 * s + step) % 128)):
                v = f if by == 0 else pltpu.roll(f, by, 1)
                sums.append(
                    tree(
                        [
                            ref[pl.ds(start + 8 * (s * 10 + 5 * m + i), 8), :] * spread(v, i)
                            for i in range(5)
                        ]
                    )
                )
        late = sums[1]
        for v in sums[2:]:
            late = late + v
        return sums[0], late

    def tile(d):
        return pl.ds(pl.multiple_of(8 * d, 8), 8)

    def inside(d):
        return (z <= d) & (z >= d - (NY - 1))

    nothing = jnp.zeros((8, 128), F32)

    def finish(work):
        for _ in work:
            pass

    def sweep(n, half, f, step, update, work=(), share=0):
        work = iter(work)
        for m in range(8):
            e = m if step == 1 else 7 - m
            d = 16 * n + 8 * half + e
            matrix = (al if step == 1 else au)[half]
            early, late = product(matrix, WIDTH * (8 * n + e), f, step)
            f = update(n, half, e, d, early, late)
            for _ in range(share):
                next(work, None)
        finish(work)
        return f

    def forward_first(n, half, e, d, early, late):
        f = jnp.where(inside(d), (g[half][pl.ds(64 * n + 8 * e, 8), :] - early) - late, 0.0)
        f1[d] = f
        return f

    def backward_first(n, half, e, d, early, late):
        f = jnp.where(inside(d), (f1[d] - early) - late, 0.0)
        f1[d] = f
        h[tile(d), :] = early + late
        return f

    def forward_second(n, half, e, d, early, late):
        f = jnp.where(inside(d), -(h[tile(d), :] + early) - late, 0.0)
        c1[d] = early + late
        return f

    def backward_second(n, half, e, d, early, late):
        f = jnp.where(inside(d), -(c1[d] + early) - late, 0.0)
        f1[d] = f1[d] + f
        change = jnp.where(inside(d), early + late, 0.0)
        by_z = pltpu.roll(change, 1, 1)
        h[tile(d + 1), :] = vv[pl.ds(d + 1, 1), :] * tree(
            [column(tf, d + 1, 75, i) * spread(change, i) for i in range(5)]
            + [column(tf, d + 1, 100, i) * spread(by_z, i) for i in range(5)]
        )
        return f

    finish(invert(0, 0))
    finish(couple_lower(0, 0))
    finish(start_values(0, 0))
    finish(invert(0, 1))

    def first_rows(n, f):
        f = sweep(
            n, 0, f, 1, forward_first,
            chain(mixed(couple_lower(n, 1), invert(n + 1, 0)), start_values(n, 1)), SHARE,
        )
        return sweep(
            n, 1, f, 1, forward_first,
            chain(mixed(couple_lower(n + 1, 0), invert(n + 1, 1)), start_values(n + 1, 0)), SHARE,
        )

    f = lax.fori_loop(0, 5, first_rows, nothing)
    f = sweep(5, 0, f, 1, forward_first, chain(couple_lower(5, 1), start_values(5, 1)), 6)
    sweep(5, 1, f, 1, forward_first, couple_upper(5, 1), 6)

    def last_rows(m, f):
        n = 5 - m
        f = sweep(n, 1, f, -1, backward_first, couple_upper(n, 0), 6)
        return sweep(n, 0, f, -1, backward_first, couple_upper(n - 1, 1), 6)

    f = lax.fori_loop(0, 5, last_rows, nothing)
    f = sweep(0, 1, f, -1, backward_first, couple_upper(0, 0), 6)
    sweep(0, 0, f, -1, backward_first)

    def again_forward(n, f):
        return sweep(n, 1, sweep(n, 0, f, 1, forward_second), 1, forward_second)

    lax.fori_loop(0, 6, again_forward, nothing)
    h[0:8, :] = nothing

    def again_backward(m, f):
        n = 5 - m
        return sweep(n, 0, sweep(n, 1, f, -1, backward_second), -1, backward_second)

    lax.fori_loop(0, 6, again_backward, nothing)

    for bit, length in ((16, 79), (8, 71), (4, 67), (2, 65), (1, 64)):
        far = (z & bit) != 0
        for d in range(length):
            f1[d] = jnp.where(far, f1[d + bit], f1[d])
            here, there = pl.ds(8 * d, 8), pl.ds(8 * (d + bit), 8)
            h[here, :] = jnp.where(far, h[there, :], h[here, :])

    owner_y = lane & 15
    owner_z = lane >> 4

    def collect(n, sums):
        sums = list(sums)
        for jy in range(2):
            y = 4 * n + 2 * side + jy
            value = f1[y]
            total = h[tile(y), :]
            for by in (16, 8, 4, 2, 1):
                total = total + pltpu.roll(total, 128 - by, 1)
            for jz in range(2):
                merged = jnp.where(sub < 5, value, pltpu.roll(total, 5 if jz == 0 else 2, 0))
                for p in range(4):
                    index = jnp.where(sub < 5, p * 32 + 4 * owner_z + 2 * core + jz, p * 32)
                    picked = jnp.take_along_axis(merged, index, axis=1)
                    k = p * 4 + jz * 2 + jy
                    sums[k] = jnp.where(owner_y == n, picked, sums[k])
        return tuple(sums)

    slots = lax.fori_loop(0, 16, collect, (nothing,) * 16, unroll=4)
    out[...] = jnp.concatenate(slots, axis=0).T


def unpack_kernel(slots, correction, coarse):
    values = slots[...].T
    gz = lax.axis_index("z") * 2 + lax.axis_index("c")
    for p in range(4):
        for jy in range(2):
            for jz in range(2):
                k = 8 * (p * 4 + jz * 2 + jy)
                correction[pl.ds(p * 4 + jy * 2 + jz, 5, stride=16), :] = values[k : k + 5]
                extra = pltpu.roll(values[k : k + 8], (128 - 8 * gz) % 128, 1)
                if jz == 0:
                    coarse[pl.ds(p * 2 + jy, 3, stride=8), :] = extra[5:8]
                else:
                    coarse[pl.ds(24 + p * 2 + jy, 2, stride=8), :] = extra[5:7]


def on_device(rhs, codes, piv, low_x, up_x, low, up, volume):
    smem = pl.BlockSpec(memory_space=SMEM)
    vmem = pl.BlockSpec(memory_space=VMEM)
    hbm = pl.BlockSpec(memory_space=pl.ANY)
    packed = pl.pallas_call(
        pack_kernel,
        out_shape=jax.ShapeDtypeStruct((128 * 24, 128), F32),
        in_specs=[smem] + [hbm] * 7,
        out_specs=vmem,
        scratch_shapes=[
            pltpu.VMEM((80, 128), F32),
            pltpu.VMEM((16, 128), jnp.int32),
            pltpu.VMEM((400, 128), F32),
            pltpu.VMEM((150, 2, 128), F32),
            pltpu.VMEM((150, 2, 128), F32),
            pltpu.VMEM((800, 128), F32),
            pltpu.VMEM((800, 128), F32),
            pltpu.VMEM((2, 128, 128), F32),
            pltpu.SemaphoreType.DMA((7,)),
        ],
        compiler_params=pltpu.CompilerParams(vmem_limit_bytes=60 << 20),
        name="pack",
    )(
        volume,
        rhs.reshape(80, 128),
        codes.reshape(16, 128),
        piv.reshape(400, 128),
        low_x.reshape(150, 2, 128),
        up_x.reshape(150, 2, 128),
        low.reshape(800, 128),
        up.reshape(800, 128),
    )
    mine = lax.all_to_all(packed.reshape(128, 24, 128), GROUP, 0, 0, tiled=True)
    other_x = lax.ppermute(mine, "xl", SWAP)
    other_c = lax.ppermute(mine, "c", SWAP)
    other_cx = lax.ppermute(other_x, "c", SWAP)
    quarters = [v.reshape(8, 16, 24, 128) for v in (mine, other_c, other_x, other_cx)]
    diag = pltpu.VMEM((96, 8, 128), F32)
    slots = pl.pallas_call(
        main_kernel,
        out_shape=jax.ShapeDtypeStruct((128, 128), F32),
        in_specs=[hbm] * 4,
        out_specs=vmem,
        scratch_shapes=[
            pltpu.VMEM((8, 2, 2, 17, 2, 8, 128), F32),
            pltpu.VMEM((8, 2, 17, 2, 8, 128), F32),
            pltpu.VMEM((98 * ROWS, 128), F32),
            pltpu.VMEM((50 * 128, 128), F32),
            pltpu.VMEM((4, 128, 128), F32),
            *[pltpu.VMEM((48 * WIDTH, 128), F32)] * 4,
            pltpu.VMEM((48 * 8, 128), F32),
            pltpu.VMEM((48 * 8, 128), F32),
            pltpu.VMEM((97 * 8, 128), F32),
            pltpu.VMEM((104, 128), F32),
            diag,
            diag,
            pltpu.VMEM((6, 100, 8, 128), F32),
            pltpu.VMEM((6, 100, 8, 128), F32),
            pltpu.SemaphoreType.DMA((12,)),
        ],
        compiler_params=pltpu.CompilerParams(vmem_limit_bytes=60 << 20),
        name="sweeps",
    )(*quarters)
    slots = lax.all_to_all(slots.reshape(128, 1, 128), GROUP, 0, 0, tiled=True)
    correction, coarse = pl.pallas_call(
        unpack_kernel,
        out_shape=(
            jax.ShapeDtypeStruct((80, 128), F32),
            jax.ShapeDtypeStruct((40, 128), F32),
        ),
        in_specs=[vmem],
        out_specs=(vmem, vmem),
        name="unpack",
    )(slots.reshape(128, 128))
    return correction.reshape(5, 4, 2, 2, 128), coarse[:, :8].reshape(5, 4, 2, 8)


def solution(mesh):
    split = Mesh(mesh.devices.reshape(8, 2, 2, 8, 2), ("cy", "xh", "xl", "z", "c"))
    gy = ("cy", "xh", "xl")
    gz = ("z", "c")
    return jax.shard_map(
        on_device,
        mesh=split,
        in_specs=(
            P(None, None, gy, gz, None),
            P(None, gy, gz, None),
            P(None, None, None, gy, gz, None),
            P(None, None, None, gy, gz, None),
            P(None, None, None, gy, gz, None),
            P(None, None, None, None, gy, gz, None),
            P(None, None, None, None, gy, gz, None),
            P(gy, gz),
        ),
        out_specs=(P(None, None, gy, gz, None), P(None, None, gy, gz)),
        check_vma=False,
    )
```

```python
from itertools import chain

import jax
import jax.numpy as jnp
from jax import lax
from jax.experimental import pallas as pl
from jax.experimental.pallas import tpu as pltpu
from jax.sharding import Mesh, PartitionSpec as P

F32 = jnp.float32
NZ = 32
NY = 64
DIAGS = NY + NZ - 1
PITCH = 272
ROWS = 145
WIDTH = 321
SHARE = 13
SWAP = [(0, 1), (1, 0)]
GROUP = ("z", "cy", "xh")
SMEM = pltpu.SMEM
VMEM = pltpu.VMEM


def tree(terms):
    terms = list(terms)
    while len(terms) > 1:
        terms = [
            terms[k] + terms[k + 1] if k + 1 < len(terms) else terms[k]
            for k in range(0, len(terms), 2)
        ]
    return terms[0]


def spread(value, i):
    return jnp.broadcast_to(value[i : i + 1, :], (8, 128))


def pack_kernel(
    vol, rhs_in, codes_in, piv_in, low_x_in, up_x_in, low_in, up_in, out,
    rhs, codes, piv, low_x, up_x, low, up, tile, sem,
):
    copies = [
        pltpu.make_async_copy(src, dst, sem.at[n])
        for n, (src, dst) in enumerate(
            (
                (piv_in, piv),
                (low_x_in, low_x),
                (up_x_in, up_x),
                (low_in, low),
                (up_in, up),
                (rhs_in, rhs),
                (codes_in, codes),
            )
        )
    ]
    for copy in copies:
        copy.start()
    for copy in copies[:4]:
        copy.wait()
    gz = lax.axis_index("z") * 2 + lax.axis_index("c")
    zero = jnp.zeros((25, 128), F32)
    component = lax.broadcasted_iota(jnp.int32, (5, 128), 0)
    for jz in range(2):
        for jy in range(2):
            for p in range(4):
                at = p * 4 + jy * 2 + jz
                t = tile.at[jy * 4 + p]
                t[0:25, :] = piv[pl.ds(at, 25, stride=16), :]
                t[25:50, :] = low_x[pl.ds(2 * p - 2 + jy, 25, stride=6), jz, :] if p > 0 else zero
                t[50:75, :] = up_x[pl.ds(2 * p + jy, 25, stride=6), jz, :] if p < 3 else zero
                t[75:100, :] = low[pl.ds(at, 25, stride=16), :]
                along_z = low[pl.ds(400 + at, 25, stride=16), :]
                if jz == 0:
                    along_z = jnp.where(gz == 0, 0.0, along_z)
                t[100:125, :] = along_z
                t[125:128, :] = zero[:3]
                out[pl.ds(jz * 8 + jy * 4 + p, 128, stride=24), :] = t[...].T
    for copy in copies[4:]:
        copy.wait()
    for jz in range(2):
        for p in range(4):
            t = tile.at[jz * 4 + p]
            for jy in range(2):
                at = p * 4 + jy * 2 + jz
                base = 64 * jy
                t[base : base + 25, :] = up[pl.ds(at, 25, stride=16), :]
                along_z = up[pl.ds(400 + at, 25, stride=16), :]
                if jz == 1:
                    along_z = jnp.where(gz == 15, 0.0, along_z)
                t[base + 25 : base + 50, :] = along_z
                code = jnp.broadcast_to(codes[at : at + 1, :], (5, 128))
                removed = ((code == 1) & (component >= 1) & (component <= 3)) | (
                    (code == 2) & (component == 3)
                )
                t[base + 50 : base + 55, :] = jnp.where(
                    removed, 0.0, rhs[pl.ds(at, 5, stride=16), :]
                )
                t[base + 55 : base + 64, :] = jnp.full((9, 128), vol[jy, jz], F32)
            out[pl.ds(16 + jz * 4 + p, 128, stride=24), :] = t[...].T


def column(ref, d, base, j):
    return ref[pl.ds(ROWS * d + base + j, 8, stride=5), :]


def matmul(left, right, into):
    for o in range(5):
        into.append([tree([left[o][i] * right[i][j] for i in range(5)]) for j in range(5)])
        yield


def mixed(*works):
    works = list(works)
    while works:
        for work in list(works):
            try:
                next(work)
            except StopIteration:
                works.remove(work)
                continue
            yield


def turned(block, by):
    return [[pltpu.roll(v, by, 1) for v in line] for line in block]


def main_kernel(
    q0, q1, q2, q3, out, df, du, tf, tu, tmp, al0, al1, au0, au1, g0, g1, h, vv, f1, c1, full0, full1, sem
):
    core = lax.axis_index("c")
    side = lax.axis_index("xl")
    copies = []
    for n, (q, dc, dx) in enumerate(((q0, 0, 0), (q1, 1, 0), (q2, 0, 1), (q3, 1, 1))):
        c = core + dc - 2 * core * dc
        x = side + dx - 2 * side * dx
        for part in range(3):
            src = q.at[:, :, pl.ds(8 * part, 8), :]
            dst = (
                df.at[:, c, part, pl.ds(0, 16), x] if part < 2 else du.at[:, c, pl.ds(0, 16), x]
            )
            copies.append(pltpu.make_async_copy(src, dst, sem.at[n * 3 + part]))
    for copy in copies[2::3]:
        copy.start()
    for part in range(2):
        for copy in copies[part::3]:
            copy.start()
    for copy in copies[2::3]:
        copy.wait()
    fl = df.reshape(32 * PITCH, 128)
    ul = du.reshape(16 * PITCH, 128)
    lane = lax.broadcasted_iota(jnp.int32, (8, 128), 1)
    sub = lax.broadcasted_iota(jnp.int32, (8, 128), 0)
    z = lane & 31
    even_z = (lane & 1) == 0

    def turn_u(n, carry):
        for k in range(8):
            e = 8 * n + k
            for p in range(4):
                for jz in range(2):
                    tmp[k, pl.ds(p * 32 + jz, 16, stride=2), :] = ul[
                        pl.ds(8 * e + jz * 4 + p, 16, stride=PITCH - 8), :
                    ]
            tu[pl.ds(pl.multiple_of(128 * e + 128, 128), 128), :] = tmp[k].T
        return carry

    lax.fori_loop(0, 6, turn_u, 0)

    for part in range(2):
        for copy in copies[part::3]:
            copy.wait()

    def turn_f(d, carry):
        block = jnp.concatenate(
            [fl[pl.ds(4 * d + p, 32, stride=PITCH - 4), :] for p in range(4)], axis=0
        )
        tf[pl.ds(ROWS * d, 128), :] = block.T
        return carry

    lax.fori_loop(0, DIAGS, turn_f, 0, unroll=19)

    def lower_rows(k, r):
        return tf[pl.ds(ROWS * 8 * k + r, 8, stride=ROWS), :]

    def upper_rows(k, r):
        even = tu[pl.ds(64 * 8 * k + 128 + r, 8, stride=64), :]
        odd = tu[pl.ds(64 * 8 * k + 64 + r, 8, stride=64), :]
        return jnp.where(even_z, even, odd)

    al, au, g, full = (al0, al1), (au0, au1), (g0, g1), (full0, full1)

    def invert(n, half):
        k = 2 * n + half
        piv, before, after = (
            [[lower_rows(k, 25 * m + 5 * o + i) for i in range(5)] for o in range(5)]
            for m in range(3)
        )
        back, ahead = [], []
        yield from matmul(piv, before, back)
        yield from matmul(piv, after, ahead)
        w = [piv]
        for _ in range(3):
            product_now = []
            yield from matmul(back, turned(w[-1], 32), product_now)
            w.append([[-v for v in line] for line in product_now])
        inverse = {3: w[3]}
        for s in (2, 1, 0, -1, -2, -3):
            below = []
            yield from matmul(ahead, turned(inverse[s + 1], 96), below)
            inverse[s] = [
                [(w[s][o][j] - below[o][j]) if s >= 0 else -below[o][j] for j in range(5)]
                for o in range(5)
            ]
        for s in range(4):
            for o in range(5):
                for i in range(5):
                    v = inverse[s][o][i]
                    if s > 0:
                        v = v + inverse[s - 4][o][i]
                    full[half][n, s * 25 + o * 5 + i] = v

    def couple(n, half, dest, rows, base):
        k = 2 * n + half
        for s in range(4):
            inverse = [[full[half][n, s * 25 + o * 5 + i] for i in range(5)] for o in range(5)]
            for m in range(2):
                for j in range(5):
                    terms = [rows(k, base + 25 * m + 5 * i + j) for i in range(5)]
                    if s > 0:
                        terms = [pltpu.roll(v, 32 * s, 1) for v in terms]
                    at = WIDTH * 8 * n + 8 * (s * 10 + 5 * m + j)
                    for o in range(5):
                        dest[half][pl.ds(at + o, 8, stride=WIDTH), :] = tree(
                            [inverse[o][i] * terms[i] for i in range(5)]
                        )
                    yield

    def couple_lower(n, half):
        return couple(n, half, al, lower_rows, 75)

    def couple_upper(n, half):
        return couple(n, half, au, upper_rows, 0)

    def start_values(n, half):
        k = 2 * n + half
        totals = [[] for _ in range(5)]
        for s in range(4):
            terms = [upper_rows(k, 50 + i) for i in range(5)]
            if s > 0:
                terms = [pltpu.roll(v, 32 * s, 1) for v in terms]
            for o in range(5):
                totals[o].append(
                    tree([full[half][n, s * 25 + o * 5 + i] * terms[i] for i in range(5)])
                )
            yield
        for o in range(5):
            g[half][pl.ds(64 * n + o, 8, stride=8), :] = tree(totals[o])
        vv[pl.ds(pl.multiple_of(8 * k, 8), 8), :] = upper_rows(k, 55)

    def product(ref, start, f, step):
        sums = []
        for s in range(4):
            for m, by in enumerate((32 * s, (32 * s + step) % 128)):
                v = f if by == 0 else pltpu.roll(f, by, 1)
                sums.append(
                    tree(
                        [
                            ref[pl.ds(start + 8 * (s * 10 + 5 * m + i), 8), :] * spread(v, i)
                            for i in range(5)
                        ]
                    )
                )
        return sums[0], tree(sums[1:])

    def tile(d):
        return pl.ds(pl.multiple_of(8 * d, 8), 8)

    def inside(d):
        return (z <= d) & (z >= d - (NY - 1))

    nothing = jnp.zeros((8, 128), F32)

    def finish(work):
        for _ in work:
            pass

    def sweep(n, half, f, step, update, work=(), share=0):
        work = iter(work)
        for m in range(8):
            e = m if step == 1 else 7 - m
            d = 16 * n + 8 * half + e
            matrix = (al if step == 1 else au)[half]
            early, late = product(matrix, WIDTH * (8 * n + e), f, step)
            f = update(n, half, e, d, early, late)
            for _ in range(share):
                next(work, None)
        finish(work)
        return f

    def forward_first(n, half, e, d, early, late):
        f = jnp.where(inside(d), (g[half][pl.ds(64 * n + 8 * e, 8), :] - early) - late, 0.0)
        f1[d] = f
        return f

    def backward_first(n, half, e, d, early, late):
        f = jnp.where(inside(d), (f1[d] - early) - late, 0.0)
        f1[d] = f
        h[tile(d), :] = early + late
        return f

    def forward_second(n, half, e, d, early, late):
        f = jnp.where(inside(d), -(h[tile(d), :] + early) - late, 0.0)
        c1[d] = early + late
        return f

    def backward_second(n, half, e, d, early, late):
        f = jnp.where(inside(d), -(c1[d] + early) - late, 0.0)
        f1[d] = f1[d] + f
        change = jnp.where(inside(d), early + late, 0.0)
        by_z = pltpu.roll(change, 1, 1)
        h[tile(d + 1), :] = vv[pl.ds(d + 1, 1), :] * tree(
            [column(tf, d + 1, 75, i) * spread(change, i) for i in range(5)]
            + [column(tf, d + 1, 100, i) * spread(by_z, i) for i in range(5)]
        )
        return f

    finish(invert(0, 0))
    finish(couple_lower(0, 0))
    finish(start_values(0, 0))
    finish(invert(0, 1))

    def first_rows(n, f):
        f = sweep(
            n, 0, f, 1, forward_first,
            chain(mixed(couple_lower(n, 1), invert(n + 1, 0)), start_values(n, 1)), SHARE,
        )
        return sweep(
            n, 1, f, 1, forward_first,
            chain(mixed(couple_lower(n + 1, 0), invert(n + 1, 1)), start_values(n + 1, 0)), SHARE,
        )

    f = lax.fori_loop(0, 5, first_rows, nothing)
    f = sweep(5, 0, f, 1, forward_first, chain(couple_lower(5, 1), start_values(5, 1)), 6)
    sweep(5, 1, f, 1, forward_first, couple_upper(5, 1), 6)

    def last_rows(m, f):
        n = 5 - m
        f = sweep(n, 1, f, -1, backward_first, couple_upper(n, 0), 6)
        return sweep(n, 0, f, -1, backward_first, couple_upper(n - 1, 1), 6)

    f = lax.fori_loop(0, 5, last_rows, nothing)
    f = sweep(0, 1, f, -1, backward_first, couple_upper(0, 0), 6)
    sweep(0, 0, f, -1, backward_first)

    def again_forward(n, f):
        return sweep(n, 1, sweep(n, 0, f, 1, forward_second), 1, forward_second)

    lax.fori_loop(0, 6, again_forward, nothing)
    h[0:8, :] = nothing

    def again_backward(m, f):
        n = 5 - m
        return sweep(n, 0, sweep(n, 1, f, -1, backward_second), -1, backward_second)

    lax.fori_loop(0, 6, again_backward, nothing)

    for bit, length in ((16, 79), (8, 71), (4, 67), (2, 65), (1, 64)):
        far = (z & bit) != 0
        for d in range(length):
            f1[d] = jnp.where(far, f1[d + bit], f1[d])
            here, there = pl.ds(8 * d, 8), pl.ds(8 * (d + bit), 8)
            h[here, :] = jnp.where(far, h[there, :], h[here, :])

    owner_y = lane & 15
    owner_z = lane >> 4

    def collect(n, sums):
        sums = list(sums)
        for jy in range(2):
            y = 4 * n + 2 * side + jy
            value = f1[y]
            total = h[tile(y), :]
            for by in (16, 8, 4, 2, 1):
                total = total + pltpu.roll(total, 128 - by, 1)
            for jz in range(2):
                merged = jnp.where(sub < 5, value, pltpu.roll(total, 5 if jz == 0 else 2, 0))
                for p in range(4):
                    index = jnp.where(sub < 5, p * 32 + 4 * owner_z + 2 * core + jz, p * 32)
                    picked = jnp.take_along_axis(merged, index, axis=1)
                    k = p * 4 + jz * 2 + jy
                    sums[k] = jnp.where(owner_y == n, picked, sums[k])
        return tuple(sums)

    slots = lax.fori_loop(0, 16, collect, (nothing,) * 16, unroll=8)
    out[...] = jnp.concatenate(slots, axis=0).T


def unpack_kernel(slots, correction, coarse):
    values = slots[...].T
    gz = lax.axis_index("z") * 2 + lax.axis_index("c")
    for p in range(4):
        for jy in range(2):
            for jz in range(2):
                k = 8 * (p * 4 + jz * 2 + jy)
                correction[pl.ds(p * 4 + jy * 2 + jz, 5, stride=16), :] = values[k : k + 5]
                extra = pltpu.roll(values[k : k + 8], (128 - 8 * gz) % 128, 1)
                if jz == 0:
                    coarse[pl.ds(p * 2 + jy, 3, stride=8), :] = extra[5:8]
                else:
                    coarse[pl.ds(24 + p * 2 + jy, 2, stride=8), :] = extra[5:7]


def on_device(rhs, codes, piv, low_x, up_x, low, up, volume):
    smem = pl.BlockSpec(memory_space=SMEM)
    vmem = pl.BlockSpec(memory_space=VMEM)
    hbm = pl.BlockSpec(memory_space=pl.ANY)
    packed = pl.pallas_call(
        pack_kernel,
        out_shape=jax.ShapeDtypeStruct((128 * 24, 128), F32),
        in_specs=[smem] + [hbm] * 7,
        out_specs=vmem,
        scratch_shapes=[
            pltpu.VMEM((80, 128), F32),
            pltpu.VMEM((16, 128), jnp.int32),
            pltpu.VMEM((400, 128), F32),
            pltpu.VMEM((150, 2, 128), F32),
            pltpu.VMEM((150, 2, 128), F32),
            pltpu.VMEM((800, 128), F32),
            pltpu.VMEM((800, 128), F32),
            pltpu.VMEM((8, 128, 128), F32),
            pltpu.SemaphoreType.DMA((7,)),
        ],
        compiler_params=pltpu.CompilerParams(vmem_limit_bytes=60 << 20),
        name="pack",
    )(
        volume,
        rhs.reshape(80, 128),
        codes.reshape(16, 128),
        piv.reshape(400, 128),
        low_x.reshape(150, 2, 128),
        up_x.reshape(150, 2, 128),
        low.reshape(800, 128),
        up.reshape(800, 128),
    )
    mine = lax.all_to_all(packed.reshape(128, 24, 128), GROUP, 0, 0, tiled=True)
    other_x = lax.ppermute(mine, "xl", SWAP)
    other_c = lax.ppermute(mine, "c", SWAP)
    other_cx = lax.ppermute(other_x, "c", SWAP)
    quarters = [v.reshape(8, 16, 24, 128) for v in (mine, other_c, other_x, other_cx)]
    diag = pltpu.VMEM((96, 8, 128), F32)
    slots = pl.pallas_call(
        main_kernel,
        out_shape=jax.ShapeDtypeStruct((128, 128), F32),
        in_specs=[hbm] * 4,
        out_specs=vmem,
        scratch_shapes=[
            pltpu.VMEM((8, 2, 2, 17, 2, 8, 128), F32),
            pltpu.VMEM((8, 2, 17, 2, 8, 128), F32),
            pltpu.VMEM((98 * ROWS, 128), F32),
            pltpu.VMEM((50 * 128, 128), F32),
            pltpu.VMEM((8, 128, 128), F32),
            *[pltpu.VMEM((48 * WIDTH, 128), F32)] * 4,
            pltpu.VMEM((48 * 8, 128), F32),
            pltpu.VMEM((48 * 8, 128), F32),
            pltpu.VMEM((97 * 8, 128), F32),
            pltpu.VMEM((104, 128), F32),
            diag,
            diag,
            pltpu.VMEM((6, 100, 8, 128), F32),
            pltpu.VMEM((6, 100, 8, 128), F32),
            pltpu.SemaphoreType.DMA((12,)),
        ],
        compiler_params=pltpu.CompilerParams(vmem_limit_bytes=60 << 20),
        name="sweeps",
    )(*quarters)
    slots = lax.all_to_all(slots.reshape(128, 1, 128), GROUP, 0, 0, tiled=True)
    correction, coarse = pl.pallas_call(
        unpack_kernel,
        out_shape=(
            jax.ShapeDtypeStruct((80, 128), F32),
            jax.ShapeDtypeStruct((40, 128), F32),
        ),
        in_specs=[vmem],
        out_specs=(vmem, vmem),
        name="unpack",
    )(slots.reshape(128, 128))
    return correction.reshape(5, 4, 2, 2, 128), coarse[:, :8].reshape(5, 4, 2, 8)


def solution(mesh):
    split = Mesh(mesh.devices.reshape(8, 2, 2, 8, 2), ("cy", "xh", "xl", "z", "c"))
    gy = ("cy", "xh", "xl")
    gz = ("z", "c")
    return jax.shard_map(
        on_device,
        mesh=split,
        in_specs=(
            P(None, None, gy, gz, None),
            P(None, gy, gz, None),
            P(None, None, None, gy, gz, None),
            P(None, None, None, gy, gz, None),
            P(None, None, None, gy, gz, None),
            P(None, None, None, None, gy, gz, None),
            P(None, None, None, None, gy, gz, None),
            P(gy, gz),
        ),
        out_specs=(P(None, None, gy, gz, None), P(None, None, gy, gz)),
        check_vma=False,
    )
```
